256 devices in a mesh: grp: 4 (over z_lo), seq: 64 (over y, z_hi, x, core).
Axes of the slice: x: 4, y: 4, z: 8 (z_hi: 2, z_lo: 4; z = z_hi * 4 + z_lo), core: 2. Of those that a mesh axis runs over, the one named last changes fastest.
Arguments:
- tokens: bfloat16 [64, 1024, 1024], P('seq', 'grp'), may hold values from -6 to 6
- lengths: int32 [64, 3], P('seq'), may hold values from 1 to 768, 1024 in all within a row
- in_gain: float32 [1024], replicated, may hold values from 0.25 to 1.75
- out_gain: float32 [1024], replicated, may hold values from 0.25 to 1.75
- w_in: bfloat16 [1024, 2560], replicated, may hold values from -0.1875 to 0.1875
- w_out: bfloat16 [1024, 1024], replicated, may hold values from -0.1875 to 0.1875
- w_qgate: float32 [1024, 8], replicated, may hold values from -0.1875 to 0.1875
- w_xgate: float32 [1024, 8], replicated, may hold values from -0.1875 to 0.1875
- item_table: bfloat16 [32768, 1024], P('seq'), may hold values from -6 to 6
- neg_owner: int32 [64, 2048, 1], P('seq', 'grp'), may hold values from 0 to 63; in each aligned block of 512 rows (0 to 511, 512 to 1023, ..., all dimensions but the last counted through in order) at most 16 rows name the same one
- neg_slot: int32 [64, 2048], P('seq', 'grp'), may hold values from 0 to 511
- pos_owner: int32 [64, 1024, 1], P('seq', 'grp'), may hold values from 0 to 63; in each aligned block of 256 rows (0 to 255, 256 to 511, ..., all dimensions but the last counted through in order) at most 8 rows name the same one
- pos_slot: int32 [64, 1024], P('seq', 'grp'), may hold values from 0 to 511
Outputs:
- losses: float32 [64, 1024], P('seq', 'grp')
- query_grad: bfloat16 [64, 1024, 1024], P('seq', 'grp')
- table_grad: float32 [32768, 1024], P('seq')
The draws below stay inside these ranges and needn't reach their ends.
Inputs may be any that keep to these rules, and one draw needn't show every extreme that they name: `neg_owner`: in the 512 rows of one device no owner is named more than 16 times, a bound that some block reaches. `pos_owner`: in the 256 rows of one device no owner is named more than 8 times, a bound that some block reaches. `lengths`: each row sums to 1024; its largest is exactly 768.
All inputs are finite; a program needn't handle non-finite values.
Results may differ from the reference program's by a relative error of at most 0.014.
Values may be sent and summed in bfloat16 or wider, within the bound.
No kernel may reach another device: no remote copies, remote signals or barrier semaphores. Data moves between devices by JAX's collectives and lax.ppermute only.
A program may use at most 128 MiB of HBM per device.

```python
import math
import jax
import jax.numpy as jnp
import numpy as np
from jax import lax

D = 1024
HEADS = 4
QKH = 64
PARTS_SIZE = 8
HIST = 3
TOK_DEV = 256
NEG_DEV = 512
ITEM_DEV = 512
SPAN = 3
STREAM = 1024
MAXLEN = 768
NITEMS = 32768
CAPN = 16
CAPP = 8
N_GRP = 4
N_SEQ = 64


def touch_ends(drawn, stream_key, smallest, top_value):
    place = [jax.random.randint(jax.random.fold_in(stream_key, axis), (), 0, length) for axis, length in enumerate(drawn.shape)]
    main_axis = drawn.shape.index(max(drawn.shape))
    beside = place[:main_axis] + [(place[main_axis] + 1) % drawn.shape[main_axis]] + place[main_axis + 1:]
    return drawn.at[tuple(place)].set(smallest).at[tuple(beside)].set(top_value)


def block_scale(rng, dims, cuts, low, high):
    loudness, own = 1.0, jax.random.fold_in(rng, 6)
    for position, parts in cuts:
        draws = jnp.exp(jax.random.uniform(jax.random.fold_in(own, position), (parts,), jnp.float32, low / len(cuts), high / len(cuts)))
        loudness = loudness * jnp.repeat(draws, dims[position] // parts).reshape([-1 if axis == position else 1 for axis in range(len(dims))])
    return loudness


def split_up(amount, total, reach, lean):
    weights = [(1 << 20) // math.isqrt(rank ** lean) + 1 for rank in range(2, amount + 1)]
    rest, counts = total - reach - (amount - 1), [1] * (amount - 1)
    while rest > 0:
        free = [i for i in range(amount - 1) if counts[i] < reach]
        whole, budget = sum([weights[i] for i in free]), rest
        for i in free:
            addition = min(reach - counts[i], max(1, budget * weights[i] // whole), rest)
            counts[i] = counts[i] + addition
            rest = rest - addition
    return np.array([reach] + counts)


def uneven(own_key, number_of, total, limit, skew):
    if number_of == 2:
        one = jax.random.randint(own_key, (), max(1, total - limit), min(limit, total - 1) + 1)
        return jnp.stack([one, total - one])
    sizes = jnp.asarray(split_up(number_of, total, limit, skew), jnp.int32)
    twos = (number_of - 1) // 2
    source_of, receiver = sizes[1:1 + 2 * twos:2], sizes[2:2 + 2 * twos:2]
    margin = jnp.minimum(source_of - 1, limit - receiver)
    moved = jax.random.randint(jax.random.fold_in(own_key, 1), (twos,), 0, 1 << 20) % (margin + 1)
    sizes = sizes.at[1:1 + 2 * twos:2].set(source_of - moved).at[2:2 + 2 * twos:2].set(receiver + moved)
    return sizes[jax.random.permutation(jax.random.fold_in(own_key, 2), number_of)]


def assign_block(stream_key, own, number, rows, count, top, limit, slope):
    sequence = jax.random.permutation(stream_key, count)
    heavy_load, usual = load_shares(count, rows * top, limit, slope, True), load_shares(count, rows * top, limit, slope, False)
    places = jnp.arange(count)

    def named(sizes, turn):
        used = int((sizes > 0).sum())
        fixed = max(1, used // 4)
        passed = fixed + (places - fixed + turn * (used - fixed)) % max(1, count - fixed)
        return jnp.zeros((count,), jnp.int32).at[sequence[jnp.where(places < fixed, places, passed)]].set(jnp.asarray(sizes, jnp.int32))

    sizes = jnp.where(number % 4 == 0, named(heavy_load, number // 4), named(usual, number - number // 4 - 1))
    mixed = jax.random.permutation(jax.random.fold_in(own, 3), count)
    source_of, taker = mixed[0:count // 2 * 2:2], mixed[1:count // 2 * 2:2]
    room = jnp.minimum(sizes[source_of] - 1, limit - sizes[taker]) // 2
    room = jnp.where((source_of == sequence[0]) | (taker == sequence[0]) | (sizes[taker] == 0), 0, jnp.maximum(room, 0))
    passed = jax.random.randint(jax.random.fold_in(own, 4), (count // 2,), 0, 1 << 20) % (room + 1)
    sizes = sizes.at[source_of].add(-passed).at[taker].add(passed)
    items = jnp.searchsorted(jnp.cumsum(sizes), jnp.arange(rows * top), side="right").astype(jnp.int32)
    grid = items.reshape(top, rows).T
    grid = grid[jax.random.permutation(jax.random.fold_in(own, 1), rows)]
    turn = jax.random.randint(jax.random.fold_in(own, 2), (rows, 1), 0, top)
    return jnp.take_along_axis(grid, (jnp.arange(top)[None, :] + turn) % top, axis=1)


def load_shares(number_of, total, bound, slope, full):
    weights = [(1 << 20) // math.isqrt(rank ** slope) + 1 for rank in range(1, number_of + 1)]
    largest = bound if full else min(bound, max(-(-total // number_of), total * weights[0] // sum(weights)))
    least = 1 if total - largest >= number_of - 1 else 0
    given, spare = [largest] + [least] * (number_of - 1), total - largest - least * (number_of - 1)
    while spare > 0:
        candidates = [i for i in range(1, number_of) if given[i] < largest] or [i for i in range(1, number_of) if given[i] < bound]
        whole, remaining = sum([weights[i] for i in candidates]), spare
        for i in candidates:
            addition = min(bound - given[i], max(1, remaining * weights[i] // whole), spare)
            given[i] = given[i] + addition
            spare = spare - addition
    return np.array(given)


def noise(own_key, dims, deviation, most, shards=(), kind=jnp.bfloat16):
    drawn = jax.random.normal(own_key, dims, jnp.float32) * deviation
    if len(shards) > 0:
        drawn = block_scale(own_key, dims, shards, -0.22, 0.18) * drawn
    return jnp.clip(drawn, min=-most, max=most).astype(kind)


def setup_inputs(seed: int = 0) -> dict:
    keys = jax.random.split(jax.random.key(seed), 14)
    tokens = noise(keys[0], (N_SEQ, STREAM, D), 1.0, 6.0, ((0, 64), (1, 4)))
    lengths = jax.vmap(lambda own: uneven(own, HIST, STREAM, MAXLEN, 2))(jax.random.split(keys[1], N_SEQ)).reshape((N_SEQ, HIST)).astype(jnp.int32)
    in_gain = jnp.clip(1.0 + 0.15 * jax.random.normal(keys[2], (D,), jnp.float32), 0.25, 1.75)
    out_gain = jnp.clip(1.0 + 0.15 * jax.random.normal(keys[3], (D,), jnp.float32), 0.25, 1.75)
    w_in = noise(keys[4], (D, 2 * D + 2 * HEADS * QKH), D ** -0.5, 0.1875)
    w_out = noise(keys[5], (D, D), D ** -0.5, 0.1875)
    w_qgate = noise(keys[6], (D, PARTS_SIZE), D ** -0.5, 0.1875, (), jnp.float32)
    w_xgate = noise(keys[7], (D, PARTS_SIZE), D ** -0.5, 0.1875, (), jnp.float32)
    item_table = noise(keys[8], (NITEMS, D), 1.0, 6.0, ((0, 64),))
    neg_owner_keys = jax.random.split(jax.random.fold_in(keys[9], 1), N_SEQ * (N_GRP * NEG_DEV) // NEG_DEV)
    neg_owner_turns = jax.random.permutation(jax.random.fold_in(keys[9], 3), N_SEQ * (N_GRP * NEG_DEV) // NEG_DEV)
    neg_owner = jax.vmap(lambda own, number: assign_block(jax.random.fold_in(keys[9], 2), own, number, NEG_DEV, N_SEQ, 1, CAPN, 2))(neg_owner_keys, neg_owner_turns).reshape((N_SEQ, N_GRP * NEG_DEV, 1))
    neg_slot = touch_ends(jax.random.randint(keys[10], (N_SEQ, N_GRP * NEG_DEV), 0, ITEM_DEV), jax.random.fold_in(keys[10], 1), 0, ITEM_DEV - 1).astype(jnp.int32)
    pos_owner_keys = jax.random.split(jax.random.fold_in(keys[11], 1), N_SEQ * STREAM // TOK_DEV)
    pos_owner_turns = jax.random.permutation(jax.random.fold_in(keys[11], 3), N_SEQ * STREAM // TOK_DEV)
    pos_owner = jax.vmap(lambda own, number: assign_block(jax.random.fold_in(keys[11], 2), own, number, TOK_DEV, N_SEQ, 1, CAPP, 2))(pos_owner_keys, pos_owner_turns).reshape((N_SEQ, STREAM, 1))
    pos_slot = touch_ends(jax.random.randint(keys[12], (N_SEQ, STREAM), 0, ITEM_DEV), jax.random.fold_in(keys[12], 1), 0, ITEM_DEV - 1).astype(jnp.int32)
    return {"tokens": tokens, "lengths": lengths, "in_gain": in_gain, "out_gain": out_gain, "w_in": w_in, "w_out": w_out, "w_qgate": w_qgate, "w_xgate": w_xgate, "item_table": item_table, "neg_owner": neg_owner, "neg_slot": neg_slot, "pos_owner": pos_owner, "pos_slot": pos_slot}


INV_TEMP = 32.0
GATE_SCALE = 2.0

def layer_norm(values, gain_vec):
    average = lax.optimization_barrier(jnp.mean(values, -1, keepdims=True))
    centred = values - average
    spread = lax.optimization_barrier(jnp.mean(centred * centred, -1, keepdims=True))
    return centred * lax.rsqrt(spread + 1e-05) * gain_vec

def segment_of(positions, lengths):
    seq_ends = jnp.cumsum(lengths)
    return lax.optimization_barrier(jnp.sum((seq_ends[None, :] <= positions[:, None]).astype(jnp.int32), 1))

def trunk_front(block_tokens, in_gain, w_in):
    normed = layer_norm(block_tokens.astype(jnp.float32), in_gain).astype(jnp.bfloat16)
    projected = jax.nn.silu(jnp.dot(normed, w_in, preferred_element_type=jnp.float32)).astype(jnp.bfloat16)
    model_width = block_tokens.shape[1]
    qk_width = (w_in.shape[1] - 2 * model_width) // 2
    return (projected[:, :model_width], projected[:, model_width:2 * model_width], projected[:, 2 * model_width:2 * model_width + qk_width], projected[:, 2 * model_width + qk_width:])

def attend(queries, keys_all, values_all, query_pos, key_pos, lengths):
    query_seg = segment_of(query_pos, lengths)
    key_seg = segment_of(key_pos, lengths)
    visible = (query_seg[:, None] == key_seg[None, :]) & (key_pos[None, :] <= query_pos[:, None]) & (key_pos[None, :] >= 0)
    q_heads = queries.reshape(queries.shape[0], HEADS, -1).astype(jnp.float32)
    k_heads = keys_all.reshape(keys_all.shape[0], HEADS, -1).astype(jnp.float32)
    v_heads = values_all.reshape(values_all.shape[0], HEADS, -1).astype(jnp.float32)
    scores = jnp.einsum('ihd,jhd->hij', q_heads, k_heads) * (1.0 / math.sqrt(QKH))
    weights = (jax.nn.silu(scores) * visible[None].astype(jnp.float32)).astype(jnp.bfloat16)
    mixed = jnp.einsum('hij,jhd->ihd', weights.astype(jnp.float32), v_heads)
    return mixed.reshape(queries.shape[0], -1)

def trunk_back(block_tokens, gate_part, mixed, out_gain, w_out):
    gated = (layer_norm(mixed, out_gain) * gate_part.astype(jnp.float32)).astype(jnp.bfloat16)
    return block_tokens.astype(jnp.float32) + jnp.dot(gated, w_out, preferred_element_type=jnp.float32)

def unit_parts(matrix_rows):
    pieces = matrix_rows.reshape(matrix_rows.shape[0], PARTS_SIZE, -1)
    return pieces * lax.rsqrt(lax.optimization_barrier(jnp.sum(pieces * pieces, -1, keepdims=True)) + 1e-06)

def gate_weights(logits):
    raised = jnp.exp(GATE_SCALE * jnp.tanh(logits))
    return raised / lax.optimization_barrier(jnp.sum(raised, 0, keepdims=True))

def block_loss(query, neg_rows, pos_rows, w_qgate, w_xgate):
    highest = lax.Precision.HIGHEST
    query_unit = unit_parts(query)
    neg_unit = unit_parts(neg_rows)
    pos_unit = unit_parts(pos_rows)
    query_gate = jnp.dot(query, w_qgate, precision=highest).T
    neg_gate = jnp.dot(neg_rows, w_xgate, precision=highest).T
    pos_gate = jnp.dot(pos_rows, w_xgate, precision=highest).T
    neg_cos = jnp.einsum('ipd,xpd->pix', query_unit, neg_unit, precision=highest)
    neg_mix = gate_weights(query_gate[:, :, None] + neg_gate[:, None, :])
    neg_logit = INV_TEMP * lax.optimization_barrier(jnp.sum(neg_mix * neg_cos, 0))
    pos_cos = lax.optimization_barrier(jnp.sum(query_unit * pos_unit, -1)).T
    pos_mix = gate_weights(query_gate + pos_gate)
    pos_logit = INV_TEMP * lax.optimization_barrier(jnp.sum(pos_mix * pos_cos, 0))
    partition = jnp.exp(pos_logit) + lax.optimization_barrier(jnp.sum(jnp.exp(neg_logit), -1))
    return jnp.log(partition) - pos_logit

def reference(tokens, lengths, in_gain, out_gain, w_in, w_out, w_qgate, w_xgate, item_table, neg_owner, neg_slot, pos_owner, pos_slot):
    streams = tokens.shape[0]
    blocks = streams * N_GRP
    qk_width = HEADS * QKH
    token_blocks = tokens.reshape(blocks, TOK_DEV, D)

    def front(block_tokens):
        return trunk_front(block_tokens, in_gain, w_in)
    gate_all, value_all, query_all, key_all = lax.map(front, token_blocks)
    key_rows = key_all.reshape(streams, N_GRP, TOK_DEV, qk_width)
    value_rows = value_all.reshape(streams, N_GRP, TOK_DEV, D)
    pad_keys = jnp.concatenate([jnp.zeros((streams, SPAN, TOK_DEV, qk_width), jnp.bfloat16), key_rows], 1)
    pad_values = jnp.concatenate([jnp.zeros((streams, SPAN, TOK_DEV, D), jnp.bfloat16), value_rows], 1)
    neg_ids = (neg_owner[:, :, 0] * ITEM_DEV + neg_slot).astype(jnp.int32).reshape(blocks, NEG_DEV)
    pos_ids = (pos_owner[:, :, 0] * ITEM_DEV + pos_slot).astype(jnp.int32).reshape(blocks, TOK_DEV)

    def one_block(total, block_at):
        row_at = block_at // N_GRP
        inner = block_at % N_GRP
        start = inner * TOK_DEV
        query_pos = start + jnp.arange(TOK_DEV, dtype=jnp.int32)
        key_pos = start - SPAN * TOK_DEV + jnp.arange((SPAN + 1) * TOK_DEV, dtype=jnp.int32)
        keys_here = lax.dynamic_slice_in_dim(pad_keys[row_at], inner, SPAN + 1, 0).reshape(-1, qk_width)
        values_here = lax.dynamic_slice_in_dim(pad_values[row_at], inner, SPAN + 1, 0).reshape(-1, D)
        mixed = attend(query_all[block_at], keys_here, values_here, query_pos, key_pos, lengths[row_at])
        query = trunk_back(token_blocks[block_at], gate_all[block_at], mixed, out_gain, w_out)
        neg_rows = item_table[neg_ids[block_at]].astype(jnp.float32)
        pos_rows = item_table[pos_ids[block_at]].astype(jnp.float32)

        def loss_of(query_in, neg_in, pos_in):
            return block_loss(query_in, neg_in, pos_in, w_qgate, w_xgate)
        block_losses, pullback = jax.vjp(loss_of, query, neg_rows, pos_rows)
        query_back, neg_back, pos_back = pullback(jnp.ones_like(block_losses))
        total = total.at[neg_ids[block_at]].add(neg_back).at[pos_ids[block_at]].add(pos_back)
        return (total, (block_losses, query_back.astype(jnp.bfloat16)))
    table_grad, (losses, query_grad) = lax.scan(one_block, jnp.zeros((NITEMS, D), jnp.float32), jnp.arange(blocks, dtype=jnp.int32))
    return (losses.reshape(streams, -1), query_grad.reshape(streams, -1, D), table_grad)
```

```python
import math

import jax
import jax.numpy as jnp
from jax import lax
from jax.experimental import pallas as pl
from jax.experimental.pallas import tpu as pltpu
from jax.sharding import Mesh
from jax.sharding import PartitionSpec as P

HEADS = 4
PARTS_SIZE = 8
INV_TEMP = 32.0
GATE_SCALE = 2.0

D = 1024
TOK = 256
NEG = 512
ITEMS = 512
CAPN = 16
CAPP = 8
CAP = CAPN + CAPP
PEERS = 32
HALF_ROWS = PEERS * CAP
QUARTER = ITEMS // 4
QKW = 256
PW = D // PARTS_SIZE
TILE = 16

PLANE = ("y", "x", "core")
SEQ = ("y", "zh", "x", "core")
COLUMN = ("zh", "grp")

F32 = jnp.float32
BF16 = jnp.bfloat16
HIGHEST = lax.Precision.HIGHEST


def matmul(a, b):
    return jnp.dot(a, b, preferred_element_type=F32)


def matmul_nt(a, b, precision=None):
    return lax.dot_general(a, b, (((1,), (1,)), ((), ())), precision=precision, preferred_element_type=F32)


def matmul_tn(a, b, precision=None):
    return lax.dot_general(a, b, (((0,), (0,)), ((), ())), precision=precision, preferred_element_type=F32)


def vmem_call(body, outs, n_smem=0, n_any=0, scratch=(), limit=50, flops=0, moved=0, name=None):
    def call(*args):
        in_specs = [pl.BlockSpec(memory_space=pltpu.SMEM)] * n_smem
        in_specs += [pl.BlockSpec(memory_space=pl.ANY)] * n_any
        in_specs += [pl.BlockSpec(memory_space=pltpu.VMEM)] * (len(args) - n_smem - n_any)
        return pl.pallas_call(
            body,
            out_shape=outs,
            in_specs=in_specs,
            out_specs=jax.tree.map(lambda _: pl.BlockSpec(memory_space=pltpu.VMEM), outs),
            scratch_shapes=list(scratch),
            compiler_params=pltpu.CompilerParams(vmem_limit_bytes=limit * 2**20),
            cost_estimate=pl.CostEstimate(flops=flops, bytes_accessed=moved, transcendentals=0),
            name=name,
        )(*args)

    return call


def pack_body(half_ref, nown_ref, nslot_ref, pown_ref, pslot_ref, ask_ref, place_ref, back_ref, owner_ref, slot_ref, sems):
    total = NEG + TOK
    pairs = (
        (nown_ref, owner_ref.at[:, :NEG]),
        (nslot_ref, slot_ref.at[:, :NEG]),
        (pown_ref, owner_ref.at[:, NEG:]),
        (pslot_ref, slot_ref.at[:, NEG:]),
    )
    copies = [pltpu.make_async_copy(a, b, sems.at[i]) for i, (a, b) in enumerate(pairs)]
    for copy in copies:
        copy.start()
    for copy in copies:
        copy.wait()
    owner = owner_ref[...]
    slot = slot_ref[...]
    lane = lax.broadcasted_iota(jnp.int32, (1, total), 1)
    positive = (lane >= NEG).astype(jnp.int32)
    far = ((owner >> 3) & 1) ^ half_ref[0]
    peer = (owner >> 4) * 8 + (owner & 7)
    key = positive * 64 + far * 32 + peer
    hot = key == lax.broadcasted_iota(jnp.int32, (128, total), 0)
    before = lax.broadcasted_iota(jnp.int32, (total, total), 0) < lax.broadcasted_iota(jnp.int32, (total, total), 1)
    counts = matmul(hot.astype(F32).astype(BF16), before.astype(F32).astype(BF16))
    rank = jnp.sum(jnp.where(hot, counts, 0.0), 0, keepdims=True).astype(jnp.int32)
    inner = rank + positive * CAPN
    column = far * CAP + inner
    peer_hot = (peer == lax.broadcasted_iota(jnp.int32, (PEERS, total), 0)).astype(F32).astype(BF16)
    here = column == lax.broadcasted_iota(jnp.int32, (2 * CAP, total), 0)
    value = slot + 1
    high = jnp.where(here, (value >> 5).astype(F32), 0.0).astype(BF16)
    low = jnp.where(here, (value & 31).astype(F32), 0.0).astype(BF16)
    ids = matmul_nt(peer_hot, high) * 32.0 + matmul_nt(peer_hot, low)
    ask_ref[...] = ids.astype(jnp.int32) - 1
    place_ref[...] = far * HALF_ROWS + peer * CAP + inner
    back_ref[...] = peer * (2 * CAP) + column


def pack(half, neg_owner, neg_slot, pos_owner, pos_slot):
    outs = (
        jax.ShapeDtypeStruct((PEERS, 2 * CAP), jnp.int32),
        jax.ShapeDtypeStruct((1, NEG + TOK), jnp.int32),
        jax.ShapeDtypeStruct((1, NEG + TOK), jnp.int32),
    )
    row = pltpu.VMEM((1, NEG + TOK), jnp.int32)
    return vmem_call(
        pack_body, outs, n_smem=1, n_any=4, scratch=[row, row, pltpu.SemaphoreType.DMA((4,))], name="pack"
    )(half, neg_owner, neg_slot, pos_owner, pos_slot)


def look_body(ids_ref, table_ref, rows_ref):
    hot = ids_ref[...] == lax.broadcasted_iota(jnp.int32, (HALF_ROWS, ITEMS), 1)
    rows_ref[...] = matmul(hot.astype(F32).astype(BF16), table_ref[...]).astype(BF16)


def look(ids, table):
    outs = jax.ShapeDtypeStruct((HALF_ROWS, D), BF16)
    return vmem_call(look_body, outs, flops=2 * HALF_ROWS * ITEMS * D, moved=4 * 2**20, name="look")(ids, table)


def relay(own):
    ups, downs = [], []
    up = down = own
    for hop in range(3):
        up = lax.ppermute(up, "grp", [(i, i + 1) for i in range(hop, 3)])
        down = lax.ppermute(down, "grp", [(i + 1, i) for i in range(3 - hop)])
        ups.append(up)
        downs.append(down)
    return [own] + ups + downs


def lay_out(grp, own_ref, up_refs, down_refs, out_ref):
    def put(at, ref):
        out_ref[pl.ds(pl.multiple_of(at * QUARTER, QUARTER), QUARTER), :] = ref[...].astype(out_ref.dtype)

    put(grp, own_ref)
    for k in range(3):
        pl.when(grp > k)(lambda k=k: put(grp - k - 1, up_refs[k]))
        pl.when(grp < 3 - k)(lambda k=k: put(grp + k + 1, down_refs[k]))


def look_far_body(grp_ref, ids_ref, own_ref, u1, u2, u3, d1, d2, d3, rows_ref, table_ref):
    lay_out(grp_ref[0], own_ref, (u1, u2, u3), (d1, d2, d3), table_ref)
    look_body(ids_ref, table_ref, rows_ref)


def look_far(grp, ids, quarters):
    outs = jax.ShapeDtypeStruct((HALF_ROWS, D), BF16)
    return vmem_call(
        look_far_body, outs, n_smem=1, scratch=[pltpu.VMEM((ITEMS, D), BF16)], flops=2 * HALF_ROWS * ITEMS * D,
        moved=4 * 2**20, name="look_far",
    )(grp, ids, *quarters)


def spread_body(grp_ref, own_ref, u1, u2, u3, d1, d2, d3, out_ref):
    lay_out(grp_ref[0], own_ref, (u1, u2, u3), (d1, d2, d3), out_ref)


def spread(grp, quarters):
    outs = jax.ShapeDtypeStruct((ITEMS, D), F32)
    return vmem_call(spread_body, outs, n_smem=1, moved=3 * 2**20, name="spread")(grp, *quarters)


def add_body(ids_ref, grads_ref, table_ref):
    for part in range(4):
        size = 2 * ITEMS // 4
        row = lax.broadcasted_iota(jnp.int32, (size, 2 * HALF_ROWS), 0) + part * size
        hot = (ids_ref[...] == row).astype(F32).astype(BF16)
        table_ref[part * size : (part + 1) * size, :] = matmul(hot, grads_ref[...]).astype(BF16)


def add_up(ids, grads):
    outs = jax.ShapeDtypeStruct((2 * ITEMS, D), BF16)
    return vmem_call(add_body, outs, flops=8 * HALF_ROWS * ITEMS * D, moved=5 * 2**20, name="add_up")(ids, grads)


def layer_norm(values, gain_vec):
    average = jnp.mean(values, -1, keepdims=True)
    centred = values - average
    spread = jnp.mean(centred * centred, -1, keepdims=True)
    return centred * lax.rsqrt(spread + 1e-05) * gain_vec


def front_body(tok_ref, gain_ref, w_ref, gq_ref, kv_ref):
    normed = layer_norm(tok_ref[...].astype(F32), gain_ref[...]).astype(BF16)

    def project(first, size):
        half = 0.5 * matmul(normed, w_ref[:, first : first + size])
        return (half + half * jnp.tanh(half)).astype(BF16)

    for at in range(0, D, 512):
        kv_ref[:, at : at + 512] = project(D + at, 512)
    kv_ref[:, D:] = project(2 * D + QKW, QKW)
    for at in range(0, D, 512):
        gq_ref[:, at : at + 512] = project(at, 512)
    gq_ref[:, D:] = project(2 * D, QKW)


def front_kernel(own_tokens, in_gain, w_in):
    out = jax.ShapeDtypeStruct((TOK, D + QKW), BF16)
    return vmem_call(front_body, (out, out), flops=14 * 10**8, moved=7 * 2**20, name="front")(own_tokens, in_gain, w_in)


def attend_body(grp_ref, len_ref, tok_ref, gq_ref, kv0_ref, kv1_ref, kv2_ref, kv3_ref, gain_ref, wout_ref, out_ref, mixed_ref):
    start = grp_ref[0] * TOK
    ends = [len_ref[0, 0]]
    for i in range(1, len_ref.shape[1]):
        ends.append(ends[-1] + len_ref[0, i])

    def segment(pos):
        return sum((pos >= end).astype(jnp.int32) for end in ends)

    query_pos = start + lax.broadcasted_iota(jnp.int32, (TOK, 1), 0)
    query_seg = segment(query_pos)
    masks = []
    for hop in range(4):
        key_pos = start - hop * TOK + lax.broadcasted_iota(jnp.int32, (1, TOK), 1)
        seen = (query_seg == segment(key_pos)) & (key_pos >= 0) & (key_pos <= query_pos)
        masks.append(jnp.where(seen, 0.5 / math.sqrt(QKW // HEADS), 0.0))
    qkh = QKW // HEADS
    vh = D // HEADS
    for head in range(HEADS):
        query = gq_ref[:, D + head * qkh : D + (head + 1) * qkh]
        acc = jnp.zeros((TOK, vh), F32)
        for hop, ref in enumerate((kv0_ref, kv1_ref, kv2_ref, kv3_ref)):
            key = ref[:, D + head * qkh : D + (head + 1) * qkh]
            value = ref[:, head * vh : (head + 1) * vh]
            scores = matmul_nt(query, key) * masks[hop]
            weights = (scores + scores * jnp.tanh(scores)).astype(BF16)
            acc = acc + matmul(weights, value)
        mixed_ref[:, head * vh : (head + 1) * vh] = acc
    gated = (layer_norm(mixed_ref[...], gain_ref[...]) * gq_ref[:, :D].astype(F32)).astype(BF16)
    out_ref[...] = tok_ref[...].astype(F32) + matmul(gated, wout_ref[...])


def attend(grp, lengths, own_tokens, gq, kvs, out_gain, w_out):
    outs = jax.ShapeDtypeStruct((TOK, D), F32)
    return vmem_call(
        attend_body, outs, n_smem=2, scratch=[pltpu.VMEM((TOK, D), F32)], flops=2 * 10**9, moved=8 * 2**20, name="attend"
    )(grp, lengths, own_tokens, gq, *kvs, out_gain, w_out)


def gate_of(u):
    t = jnp.tanh(u)
    return t, jnp.exp(GATE_SCALE * t)


def split(values):
    high = values.astype(BF16).astype(F32)
    return high, values - high


def split_rows(values):
    high, rest = split(values)
    middle, low = split(rest)
    return jnp.concatenate([high, middle, low], 0).astype(BF16)


def loss_body(
    query_ref, near_ref, far_ref, place_ref, back_ref, wqt_ref, wxt_ref,
    loss_ref, qgrad_ref, grads_ref,
    x_ref, unit_ref, cos_ref, dcos_ref, dcosr_ref, side_ref, dqgate_ref, dxgate_ref, dx_ref, du_ref,
):
    lanes = lax.broadcasted_iota(jnp.int32, (NEG + TOK, HALF_ROWS), 1)
    hot_near = (place_ref[...] == lanes).astype(F32).astype(BF16)
    hot_far = (place_ref[...] == lanes + HALF_ROWS).astype(F32).astype(BF16)
    x_ref[...] = (matmul(hot_near, near_ref[...]) + matmul(hot_far, far_ref[...])).astype(BF16)

    part_of = lax.broadcasted_iota(jnp.int32, (16, D), 1) // PW
    pick = (part_of == lax.broadcasted_iota(jnp.int32, (16, D), 0)).astype(F32).astype(BF16)
    eye = lax.broadcasted_iota(jnp.int32, (1, PARTS_SIZE), 1)

    rows = x_ref[...].astype(F32)
    high, low = split(rows * rows)
    squares = matmul_nt(high.astype(BF16), pick) + matmul_nt(low.astype(BF16), pick)
    x_norms = lax.rsqrt(squares[:, :PARTS_SIZE] + 1e-06)
    terms = matmul_nt(x_ref[...], split_rows(wxt_ref[...]))
    xgate = terms[:, :8] + terms[:, 8:16] + terms[:, 16:]
    side = jnp.concatenate([xgate[:NEG], x_norms[:NEG], jnp.zeros((NEG, 112), F32)], 1)
    side_ref[...] = jnp.transpose(side)[:16, :]
    pgate = xgate[NEG:]

    query = query_ref[...]
    qgate = matmul_nt(query, wqt_ref[...], HIGHEST)

    pos_cos = jnp.zeros((TOK, PARTS_SIZE), F32)
    q_norms = []
    for p in range(PARTS_SIZE):
        cols = slice(p * PW, (p + 1) * PW)
        q_p = query_ref[:, cols]
        q_norm = lax.rsqrt(jnp.sum(q_p * q_p, -1, keepdims=True) + 1e-06)
        q_unit = q_p * q_norm
        unit_ref[:, cols] = q_unit
        q_high, q_low = split(q_unit)
        x_p = x_ref[:NEG, cols]
        q_two = jnp.concatenate([q_high.astype(BF16), q_low.astype(BF16)], 1)
        cos_ref[p] = matmul_nt(q_two, jnp.concatenate([x_p, x_p], 1)) * side_ref[8 + p : 9 + p, :]
        dot_p = jnp.sum(q_unit * x_ref[NEG:, cols].astype(F32), -1, keepdims=True)
        pos_cos = jnp.where(eye == p, dot_p, pos_cos)
        q_norms.append(q_norm)
    pos_cos = pos_cos * x_norms[NEG:]

    t_pos, e_pos = gate_of(qgate + pgate)
    mix_pos = e_pos / jnp.sum(e_pos, -1, keepdims=True)
    mean_pos = jnp.sum(mix_pos * pos_cos, -1, keepdims=True)
    pos_logit = INV_TEMP * mean_pos
    raised_pos = jnp.exp(pos_logit)

    dxgate_ref[...] = jnp.zeros_like(dxgate_ref)
    dqgate_ref[...] = qgate
    loss_ref[...] = raised_pos

    def tile(i, carry):
        rows = pl.ds(pl.multiple_of(i * TILE, TILE), TILE)
        qg = dqgate_ref[rows, :]
        qgs = [jnp.broadcast_to(qg[:, p : p + 1], (TILE, PW)) for p in range(PARTS_SIZE)]
        sums = [jnp.zeros((TILE, PW), F32) for _ in range(PARTS_SIZE)]
        part = jnp.zeros((TILE, PW), F32)
        for block in range(NEG // PW):
            cols = slice(block * PW, (block + 1) * PW)
            ts, es, cs = [], [], []
            total = jnp.zeros((TILE, PW), F32)
            mixed = jnp.zeros((TILE, PW), F32)
            for p in range(PARTS_SIZE):
                t, e = gate_of(qgs[p] + side_ref[p : p + 1, cols])
                c = cos_ref[p, rows, cols]
                total = total + e
                mixed = mixed + e * c
                ts.append(t)
                es.append(e)
                cs.append(c)
            inverse = 1.0 / total
            mean = mixed * inverse
            raised = jnp.exp(INV_TEMP * mean)
            part = part + raised
            scaled = raised * inverse
            for p in range(PARTS_SIZE):
                dcos = scaled * es[p]
                du = dcos * (cs[p] - mean) * (1.0 - ts[p] * ts[p])
                dcos_ref[p, rows, cols] = dcos.astype(BF16)
                dcosr_ref[p, rows, cols] = (dcos * side_ref[8 + p : 9 + p, cols]).astype(BF16)
                du_ref[p, :, cols] = du
                sums[p] = sums[p] + du
        partition = loss_ref[rows, :] + jnp.sum(part, -1, keepdims=True)
        factor = (GATE_SCALE * INV_TEMP) / partition
        dq = jnp.zeros((TILE, PARTS_SIZE), F32)
        for p in range(PARTS_SIZE):
            du = du_ref[p] * factor
            dxgate_ref[p] += du[:8] + du[8:]
            dq = jnp.where(eye == p, jnp.sum(sums[p], -1, keepdims=True), dq)
        dqgate_ref[rows, :] = dq * factor
        loss_ref[rows, :] = partition
        return carry

    lax.fori_loop(0, TOK // TILE, tile, 0, unroll=2)

    partition = loss_ref[...]
    loss_ref[...] = jnp.log(partition) - pos_logit
    share = INV_TEMP / partition
    dpos = INV_TEMP * (raised_pos / partition - 1.0)
    dcos_pos = dpos * mix_pos
    du_pos = dcos_pos * (pos_cos - mean_pos) * (GATE_SCALE - GATE_SCALE * t_pos * t_pos)
    dxgate = jnp.transpose(jnp.concatenate([jnp.sum(dxgate_ref[...], 1), jnp.zeros((120, NEG), F32)], 0))

    def by_gate(values):
        high, low = split(values)
        return jnp.concatenate([high, low, high], 1).astype(BF16)

    def gate_weights(values):
        high, low = split(values)
        return jnp.concatenate([high, high, low], 0).astype(BF16)

    dqgate = by_gate(dqgate_ref[...] + du_pos)
    dxgate = by_gate(jnp.concatenate([dxgate[:, :PARTS_SIZE], du_pos], 0))
    wq = gate_weights(wqt_ref[...])
    wx = gate_weights(wxt_ref[...])

    for p in range(PARTS_SIZE):
        cols = slice(p * PW, (p + 1) * PW)
        q_unit = unit_ref[:, cols]
        dc = dcos_pos[:, p : p + 1]
        p_norm = x_norms[NEG:, p : p + 1]
        p_unit = x_ref[NEG:, cols].astype(F32) * p_norm
        d_unit = matmul(dcosr_ref[p], x_ref[:NEG, cols]) * share + dc * p_unit
        along = jnp.sum(d_unit * q_unit, -1, keepdims=True)
        qgrad_ref[:, cols] = (q_norms[p] * (d_unit - q_unit * along) + matmul(dqgate, wq[:, cols])).astype(BF16)

        gate_term = matmul(dxgate, wx[:, cols])
        dpos_p = p_norm * dc * (q_unit - p_unit * pos_cos[:, p : p + 1]) + gate_term[NEG:]
        dx_ref[NEG:, cols] = dpos_p.astype(BF16)

        x_norm = x_norms[:NEG, p : p + 1]
        x_unit = x_ref[:NEG, cols].astype(F32) * x_norm
        d_unit = matmul_tn(dcos_ref[p], (q_unit * share).astype(BF16))
        along = jnp.sum(d_unit * x_unit, -1, keepdims=True)
        dx_ref[:NEG, cols] = (x_norm * (d_unit - x_unit * along) + gate_term[:NEG]).astype(BF16)

    for part in range(4):
        size = 2 * HALF_ROWS // 4
        row = lax.broadcasted_iota(jnp.int32, (size, NEG + TOK), 0) + part * size
        hot = (back_ref[...] == row).astype(F32).astype(BF16)
        grads_ref[part * size : (part + 1) * size, :] = matmul(hot, dx_ref[...]).astype(BF16)


def loss_and_grads(query, near, far, place, back, w_qgate, w_xgate):
    outs = (
        jax.ShapeDtypeStruct((TOK, 1), F32),
        jax.ShapeDtypeStruct((TOK, D), BF16),
        jax.ShapeDtypeStruct((2 * HALF_ROWS, D), BF16),
    )
    scratch = [
        pltpu.VMEM((NEG + TOK, D), BF16),
        pltpu.VMEM((TOK, D), F32),
        pltpu.VMEM((PARTS_SIZE, TOK, NEG), F32),
        pltpu.VMEM((PARTS_SIZE, TOK, NEG), BF16),
        pltpu.VMEM((PARTS_SIZE, TOK, NEG), BF16),
        pltpu.VMEM((2 * PARTS_SIZE, NEG), F32),
        pltpu.VMEM((TOK, PARTS_SIZE), F32),
        pltpu.VMEM((PARTS_SIZE, 8, NEG), F32),
        pltpu.VMEM((NEG + TOK, D), BF16),
        pltpu.VMEM((PARTS_SIZE, TILE, NEG), F32),
    ]
    return vmem_call(loss_body, outs, scratch=scratch, flops=8 * 10**9, moved=10 * 2**20, name="loss")(
        query, near, far, place.reshape(-1, 1), back, w_qgate.T, w_xgate.T
    )


def local(
    tokens,
    lengths,
    in_gain,
    out_gain,
    w_in,
    w_out,
    w_qgate,
    w_xgate,
    item_table,
    neg_owner,
    neg_slot,
    pos_owner,
    pos_slot,
):
    own_tokens = tokens[0]
    half = lax.axis_index("zh").astype(jnp.int32)[None]
    grp = lax.axis_index("grp").astype(jnp.int32)[None]
    barrier = lax.optimization_barrier

    moved = lax.dynamic_slice_in_dim(item_table, grp[0] * QUARTER, QUARTER, 0)
    half_then, _ = barrier((half, moved))
    moved = lax.ppermute(moved, "zh", [(0, 1), (1, 0)])

    ask, place, back = pack(
        half_then,
        neg_owner.reshape(1, NEG),
        neg_slot.reshape(1, NEG),
        pos_owner.reshape(1, TOK),
        pos_slot.reshape(1, TOK),
    )
    asked = lax.all_to_all(ask, PLANE, split_axis=0, concat_axis=0, tiled=True)

    gate_query, key_value = front_kernel(own_tokens, in_gain[None], w_in)
    kvs = [key_value]
    for hop in range(3):
        kvs.append(lax.ppermute(kvs[-1], "grp", [(i, i + 1) for i in range(3)]))
    quarters = relay(moved)

    asked_then, _, _ = barrier((asked, key_value, moved))
    near_ids = asked_then[:, :CAP].reshape(-1, 1)
    far_ids = asked_then[:, CAP:].reshape(-1, 1)
    near = lax.all_to_all(look(near_ids, item_table), PLANE, split_axis=0, concat_axis=0, tiled=True)
    far_ids, _ = barrier((far_ids, kvs[2]))
    far = lax.all_to_all(look_far(grp, far_ids, quarters), PLANE, split_axis=0, concat_axis=0, tiled=True)

    query = attend(grp, lengths, own_tokens, gate_query, kvs, out_gain[None], w_out)

    losses, query_grad, grads = loss_and_grads(query, near, far, place, back, w_qgate, w_xgate)

    came = lax.all_to_all(grads, PLANE, split_axis=0, concat_axis=0, tiled=True)
    shard = half[0] ^ (lax.broadcasted_iota(jnp.int32, asked.shape, 1) // CAP)
    rows = jnp.where(asked >= 0, asked + shard * ITEMS, -1).reshape(1, -1)
    table = add_up(rows, came)
    table = lax.psum_scatter(table, COLUMN, tiled=True)
    return (losses.reshape(1, TOK), query_grad[None], spread(grp, relay(table)))


def solution(mesh):
    fine = Mesh(mesh.devices.reshape(4, 4, 2, 4, 2), ("grp", "y", "zh", "x", "core"))
    in_specs = (
        P(SEQ, "grp", None),
        P(SEQ, None),
        P(),
        P(),
        P(),
        P(),
        P(),
        P(),
        P(SEQ, None),
        P(SEQ, "grp", None),
        P(SEQ, "grp"),
        P(SEQ, "grp", None),
        P(SEQ, "grp"),
    )
    out_specs = (P(SEQ, "grp"), P(SEQ, "grp", None), P(SEQ, None))
    return jax.shard_map(local, mesh=fine, in_specs=in_specs, out_specs=out_specs, check_vma=False)
```

```python
import math

import jax
import jax.numpy as jnp
from jax import lax
from jax.experimental import pallas as pl
from jax.experimental.pallas import tpu as pltpu
from jax.sharding import Mesh
from jax.sharding import PartitionSpec as P

HEADS = 4
PARTS_SIZE = 8
INV_TEMP = 32.0
GATE_SCALE = 2.0

D = 1024
TOK = 256
NEG = 512
ITEMS = 512
CAPN = 16
CAPP = 8
CAP = CAPN + CAPP
PEERS = 32
HALF_ROWS = PEERS * CAP
QUARTER = ITEMS // 4
WIDTHS = (512, 512)
ATTEND_COST = 8 * 10**9
QKW = 256
PW = D // PARTS_SIZE
TILE = 16

PLANE = ("y", "x", "core")
SEQ = ("y", "zh", "x", "core")
COLUMN = ("zh", "grp")

F32 = jnp.float32
BF16 = jnp.bfloat16
HIGHEST = lax.Precision.HIGHEST


def matmul(a, b):
    return jnp.dot(a, b, preferred_element_type=F32)


def matmul_nt(a, b, precision=None):
    return lax.dot_general(a, b, (((1,), (1,)), ((), ())), precision=precision, preferred_element_type=F32)


def matmul_tn(a, b, precision=None):
    return lax.dot_general(a, b, (((0,), (0,)), ((), ())), precision=precision, preferred_element_type=F32)


def vmem_call(body, outs, n_smem=0, n_any=0, scratch=(), limit=50, flops=0, moved=0, name=None):
    def call(*args):
        in_specs = [pl.BlockSpec(memory_space=pltpu.SMEM)] * n_smem
        in_specs += [pl.BlockSpec(memory_space=pl.ANY)] * n_any
        in_specs += [pl.BlockSpec(memory_space=pltpu.VMEM)] * (len(args) - n_smem - n_any)
        return pl.pallas_call(
            body,
            out_shape=outs,
            in_specs=in_specs,
            out_specs=jax.tree.map(lambda _: pl.BlockSpec(memory_space=pltpu.VMEM), outs),
            scratch_shapes=list(scratch),
            compiler_params=pltpu.CompilerParams(vmem_limit_bytes=limit * 2**20),
            cost_estimate=pl.CostEstimate(flops=flops, bytes_accessed=moved, transcendentals=0),
            name=name,
        )(*args)

    return call


def pack_body(half_ref, nown_ref, nslot_ref, pown_ref, pslot_ref, ask_ref, place_ref, back_ref, owner_ref, slot_ref, sems):
    total = NEG + TOK
    pairs = (
        (nown_ref, owner_ref.at[:, :NEG]),
        (nslot_ref, slot_ref.at[:, :NEG]),
        (pown_ref, owner_ref.at[:, NEG:]),
        (pslot_ref, slot_ref.at[:, NEG:]),
    )
    copies = [pltpu.make_async_copy(a, b, sems.at[i]) for i, (a, b) in enumerate(pairs)]
    for copy in copies:
        copy.start()
    for copy in copies:
        copy.wait()
    owner = owner_ref[...]
    slot = slot_ref[...]
    lane = lax.broadcasted_iota(jnp.int32, (1, total), 1)
    positive = (lane >= NEG).astype(jnp.int32)
    far = ((owner >> 3) & 1) ^ half_ref[0]
    peer = (owner >> 4) * 8 + (owner & 7)
    key = positive * 64 + far * 32 + peer
    hot = key == lax.broadcasted_iota(jnp.int32, (128, total), 0)
    before = lax.broadcasted_iota(jnp.int32, (total, total), 0) < lax.broadcasted_iota(jnp.int32, (total, total), 1)
    counts = matmul(hot.astype(F32).astype(BF16), before.astype(F32).astype(BF16))
    rank = jnp.sum(jnp.where(hot, counts, 0.0), 0, keepdims=True).astype(jnp.int32)
    inner = rank + positive * CAPN
    column = far * CAP + inner
    peer_hot = (peer == lax.broadcasted_iota(jnp.int32, (PEERS, total), 0)).astype(F32).astype(BF16)
    here = column == lax.broadcasted_iota(jnp.int32, (2 * CAP, total), 0)
    value = slot + 1
    high = jnp.where(here, (value >> 5).astype(F32), 0.0).astype(BF16)
    low = jnp.where(here, (value & 31).astype(F32), 0.0).astype(BF16)
    ids = matmul_nt(peer_hot, high) * 32.0 + matmul_nt(peer_hot, low)
    ask_ref[...] = ids.astype(jnp.int32) - 1
    place_ref[...] = far * HALF_ROWS + peer * CAP + inner
    back_ref[...] = peer * (2 * CAP) + column


def pack(half, neg_owner, neg_slot, pos_owner, pos_slot):
    outs = (
        jax.ShapeDtypeStruct((PEERS, 2 * CAP), jnp.int32),
        jax.ShapeDtypeStruct((1, NEG + TOK), jnp.int32),
        jax.ShapeDtypeStruct((1, NEG + TOK), jnp.int32),
    )
    row = pltpu.VMEM((1, NEG + TOK), jnp.int32)
    return vmem_call(
        pack_body, outs, n_smem=1, n_any=4, scratch=[row, row, pltpu.SemaphoreType.DMA((4,))], name="pack"
    )(half, neg_owner, neg_slot, pos_owner, pos_slot)


def look_body(ids_ref, table_ref, rows_ref):
    hot = ids_ref[...] == lax.broadcasted_iota(jnp.int32, (HALF_ROWS, ITEMS), 1)
    rows_ref[...] = matmul(hot.astype(F32).astype(BF16), table_ref[...]).astype(BF16)


def look(ids, table, cost=1):
    outs = jax.ShapeDtypeStruct((HALF_ROWS, D), BF16)
    return vmem_call(look_body, outs, flops=cost * 2 * HALF_ROWS * ITEMS * D, moved=4 * 2**20, name="look")(ids, table)


def relay(own):
    moved = [lax.ppermute(own, "grp", [(i, (i + k) % 4) for i in range(4)]) for k in (1, 2, 3)]
    return [own] + moved


def lay_out(grp, refs, out_ref, cols):
    for k, ref in enumerate(refs):
        at = ((grp - k) & 3) * QUARTER
        out_ref[pl.ds(pl.multiple_of(at, QUARTER), QUARTER), cols] = ref[...].astype(out_ref.dtype)


def spread_body(grp_ref, *refs):
    out_ref = refs[-1]
    at = 0
    for i, width in enumerate(WIDTHS):
        lay_out(grp_ref[0], refs[4 * i : 4 * i + 4], out_ref, slice(at, at + width))
        at += width


def spread(grp, quarters):
    outs = jax.ShapeDtypeStruct((ITEMS, D), F32)
    return vmem_call(spread_body, outs, n_smem=1, moved=3 * 2**20, name="spread")(grp, *quarters)


def add_body(place_ref, ids_ref, grads_ref, out_ref, *piece_refs):
    eighth = 2 * ITEMS // 8
    for pair in range(4):
        row = lax.broadcasted_iota(jnp.int32, (2 * eighth, 2 * HALF_ROWS), 0) + pair * 2 * eighth
        hot = (ids_ref[...] == row).astype(F32).astype(BF16)
        summed = matmul(hot, grads_ref[...]).astype(BF16)
        for i in range(2):
            k = 2 * pair + i
            rows = slice(i * eighth, (i + 1) * eighth)
            at = pl.multiple_of(((place_ref[0] + k) & 7) * eighth, eighth)
            out_ref[pl.ds(at, eighth), :] = summed[rows, : WIDTHS[0]]
            piece_refs[k][...] = summed[rows, WIDTHS[0] :]


def add_up(place, ids, grads):
    outs = (jax.ShapeDtypeStruct((2 * ITEMS, WIDTHS[0]), BF16),)
    outs += (jax.ShapeDtypeStruct((ITEMS // 4, WIDTHS[1]), BF16),) * 8
    return vmem_call(add_body, outs, n_smem=1, flops=8 * HALF_ROWS * ITEMS * D, moved=5 * 2**20, name="add_up")(
        place, ids, grads
    )


def ring_sum(pieces):
    def hop(value, step):
        place = [(i % 4) * 2 + i // 4 for i in range(8)]
        pairs = [(place[i], place[(i + step) % 8]) for i in range(8)]
        return lax.ppermute(value, ("grp", "zh"), pairs)

    def plus(value, piece):
        return (value.astype(F32) + piece.astype(F32)).astype(BF16)

    back = hop(pieces[4], -1)
    ahead = hop(pieces[3], 1)
    back = hop(plus(back, pieces[5]), -1)
    ahead = hop(plus(ahead, pieces[2]), 1)
    back = hop(plus(back, pieces[6]), -1)
    ahead = hop(plus(ahead, pieces[1]), 1)
    back = hop(plus(back, pieces[7]), -1)
    return (pieces[0].astype(F32) + back.astype(F32) + ahead.astype(F32)).astype(BF16)


def layer_norm(values, gain_vec):
    average = jnp.mean(values, -1, keepdims=True)
    centred = values - average
    spread = jnp.mean(centred * centred, -1, keepdims=True)
    return centred * lax.rsqrt(spread + 1e-05) * gain_vec


def front_body(tok_ref, gain_ref, w_ref, gq_ref, kv_ref):
    normed = layer_norm(tok_ref[...].astype(F32), gain_ref[...]).astype(BF16)

    def project(first, size):
        half = 0.5 * matmul(normed, w_ref[:, first : first + size])
        return (half + half * jnp.tanh(half)).astype(BF16)

    for at in range(0, D, 512):
        kv_ref[:, at : at + 512] = project(D + at, 512)
    kv_ref[:, D:] = project(2 * D + QKW, QKW)
    for at in range(0, D, 512):
        gq_ref[:, at : at + 512] = project(at, 512)
    gq_ref[:, D:] = project(2 * D, QKW)


def front_kernel(own_tokens, in_gain, w_in):
    out = jax.ShapeDtypeStruct((TOK, D + QKW), BF16)
    return vmem_call(front_body, (out, out), flops=14 * 10**8, moved=7 * 2**20, name="front")(own_tokens, in_gain, w_in)


def attend_body(grp_ref, len_ref, tok_ref, gq_ref, kv0_ref, kv1_ref, kv2_ref, kv3_ref, gain_ref, wout_ref, out_ref, mixed_ref):
    start = grp_ref[0] * TOK
    ends = [len_ref[0, 0]]
    for i in range(1, len_ref.shape[1]):
        ends.append(ends[-1] + len_ref[0, i])

    def segment(pos):
        return sum((pos >= end).astype(jnp.int32) for end in ends)

    query_pos = start + lax.broadcasted_iota(jnp.int32, (TOK, 1), 0)
    query_seg = segment(query_pos)
    masks = []
    for hop in range(4):
        key_pos = start - hop * TOK + lax.broadcasted_iota(jnp.int32, (1, TOK), 1)
        seen = (query_seg == segment(key_pos)) & (key_pos >= 0) & (key_pos <= query_pos)
        masks.append(jnp.where(seen, 0.5 / math.sqrt(QKW // HEADS), 0.0))
    qkh = QKW // HEADS
    vh = D // HEADS
    for head in range(HEADS):
        query = gq_ref[:, D + head * qkh : D + (head + 1) * qkh]
        acc = jnp.zeros((TOK, vh), F32)
        for hop, ref in enumerate((kv0_ref, kv1_ref, kv2_ref, kv3_ref)):
            key = ref[:, D + head * qkh : D + (head + 1) * qkh]
            value = ref[:, head * vh : (head + 1) * vh]
            scores = matmul_nt(query, key) * masks[hop]
            weights = (scores + scores * jnp.tanh(scores)).astype(BF16)
            acc = acc + matmul(weights, value)
        mixed_ref[:, head * vh : (head + 1) * vh] = acc
    gated = (layer_norm(mixed_ref[...], gain_ref[...]) * gq_ref[:, :D].astype(F32)).astype(BF16)
    out_ref[...] = tok_ref[...].astype(F32) + matmul(gated, wout_ref[...])


def attend(grp, lengths, own_tokens, gq, kvs, out_gain, w_out):
    outs = jax.ShapeDtypeStruct((TOK, D), F32)
    return vmem_call(
        attend_body, outs, n_smem=2, scratch=[pltpu.VMEM((TOK, D), F32)], flops=ATTEND_COST, moved=8 * 2**20, name="attend"
    )(grp, lengths, own_tokens, gq, *kvs, out_gain, w_out)


def gate_of(u):
    t = jnp.tanh(u)
    return t, jnp.exp(GATE_SCALE * t)


def split(values):
    high = values.astype(BF16).astype(F32)
    return high, values - high


def split_rows(values):
    high, rest = split(values)
    middle, low = split(rest)
    return jnp.concatenate([high, middle, low], 0).astype(BF16)


def loss_body(
    query_ref, near_ref, far_ref, place_ref, back_ref, wqt_ref, wxt_ref,
    loss_ref, qgrad_ref, grads_ref,
    x_ref, unit_ref, cos_ref, dcos_ref, dcosr_ref, side_ref, dqgate_ref, dxgate_ref, dx_ref, du_ref,
):
    lanes = lax.broadcasted_iota(jnp.int32, (NEG + TOK, HALF_ROWS), 1)
    hot_near = (place_ref[...] == lanes).astype(F32).astype(BF16)
    hot_far = (place_ref[...] == lanes + HALF_ROWS).astype(F32).astype(BF16)
    x_ref[...] = (matmul(hot_near, near_ref[...]) + matmul(hot_far, far_ref[...])).astype(BF16)

    part_of = lax.broadcasted_iota(jnp.int32, (16, D), 1) // PW
    pick = (part_of == lax.broadcasted_iota(jnp.int32, (16, D), 0)).astype(F32).astype(BF16)
    eye = lax.broadcasted_iota(jnp.int32, (1, PARTS_SIZE), 1)

    rows = x_ref[...].astype(F32)
    high, low = split(rows * rows)
    squares = matmul_nt(high.astype(BF16), pick) + matmul_nt(low.astype(BF16), pick)
    x_norms = lax.rsqrt(squares[:, :PARTS_SIZE] + 1e-06)
    terms = matmul_nt(x_ref[...], split_rows(wxt_ref[...]))
    xgate = terms[:, :8] + terms[:, 8:16] + terms[:, 16:]
    side = jnp.concatenate([xgate[:NEG], x_norms[:NEG], jnp.zeros((NEG, 112), F32)], 1)
    side_ref[...] = jnp.transpose(side)[:16, :]
    pgate = xgate[NEG:]

    query = query_ref[...]
    qgate = matmul_nt(query, wqt_ref[...], HIGHEST)

    pos_cos = jnp.zeros((TOK, PARTS_SIZE), F32)
    q_norms = []
    for p in range(PARTS_SIZE):
        cols = slice(p * PW, (p + 1) * PW)
        q_p = query_ref[:, cols]
        q_norm = lax.rsqrt(jnp.sum(q_p * q_p, -1, keepdims=True) + 1e-06)
        q_unit = q_p * q_norm
        unit_ref[:, cols] = q_unit
        q_high, q_low = split(q_unit)
        x_p = x_ref[:NEG, cols]
        q_two = jnp.concatenate([q_high.astype(BF16), q_low.astype(BF16)], 1)
        cos_ref[p] = matmul_nt(q_two, jnp.concatenate([x_p, x_p], 1)) * side_ref[8 + p : 9 + p, :]
        dot_p = jnp.sum(q_unit * x_ref[NEG:, cols].astype(F32), -1, keepdims=True)
        pos_cos = jnp.where(eye == p, dot_p, pos_cos)
        q_norms.append(q_norm)
    pos_cos = pos_cos * x_norms[NEG:]

    t_pos, e_pos = gate_of(qgate + pgate)
    mix_pos = e_pos / jnp.sum(e_pos, -1, keepdims=True)
    mean_pos = jnp.sum(mix_pos * pos_cos, -1, keepdims=True)
    pos_logit = INV_TEMP * mean_pos
    raised_pos = jnp.exp(pos_logit)

    dxgate_ref[...] = jnp.zeros_like(dxgate_ref)
    dqgate_ref[...] = qgate
    loss_ref[...] = raised_pos

    def tile(i, carry):
        rows = pl.ds(pl.multiple_of(i * TILE, TILE), TILE)
        qg = dqgate_ref[rows, :]
        qgs = [jnp.broadcast_to(qg[:, p : p + 1], (TILE, PW)) for p in range(PARTS_SIZE)]
        sums = [jnp.zeros((TILE, PW), F32) for _ in range(PARTS_SIZE)]
        part = jnp.zeros((TILE, PW), F32)
        for block in range(NEG // PW):
            cols = slice(block * PW, (block + 1) * PW)
            ts, es, cs = [], [], []
            total = jnp.zeros((TILE, PW), F32)
            mixed = jnp.zeros((TILE, PW), F32)
            for p in range(PARTS_SIZE):
                t, e = gate_of(qgs[p] + side_ref[p : p + 1, cols])
                c = cos_ref[p, rows, cols]
                total = total + e
                mixed = mixed + e * c
                ts.append(t)
                es.append(e)
                cs.append(c)
            inverse = 1.0 / total
            mean = mixed * inverse
            raised = jnp.exp(INV_TEMP * mean)
            part = part + raised
            scaled = raised * inverse
            for p in range(PARTS_SIZE):
                dcos = scaled * es[p]
                du = dcos * (cs[p] - mean) * (1.0 - ts[p] * ts[p])
                dcos_ref[p, rows, cols] = dcos.astype(BF16)
                dcosr_ref[p, rows, cols] = (dcos * side_ref[8 + p : 9 + p, cols]).astype(BF16)
                du_ref[p, :, cols] = du
                sums[p] = sums[p] + du
        partition = loss_ref[rows, :] + jnp.sum(part, -1, keepdims=True)
        factor = (GATE_SCALE * INV_TEMP) / partition
        dq = jnp.zeros((TILE, PARTS_SIZE), F32)
        for p in range(PARTS_SIZE):
            du = du_ref[p] * factor
            dxgate_ref[p] += du[:8] + du[8:]
            dq = jnp.where(eye == p, jnp.sum(sums[p], -1, keepdims=True), dq)
        dqgate_ref[rows, :] = dq * factor
        loss_ref[rows, :] = partition
        return carry

    lax.fori_loop(0, TOK // TILE, tile, 0, unroll=2)

    partition = loss_ref[...]
    loss_ref[...] = jnp.log(partition) - pos_logit
    share = INV_TEMP / partition
    dpos = INV_TEMP * (raised_pos / partition - 1.0)
    dcos_pos = dpos * mix_pos
    du_pos = dcos_pos * (pos_cos - mean_pos) * (GATE_SCALE - GATE_SCALE * t_pos * t_pos)
    dxgate = jnp.transpose(jnp.concatenate([jnp.sum(dxgate_ref[...], 1), jnp.zeros((120, NEG), F32)], 0))

    def by_gate(values):
        high, low = split(values)
        return jnp.concatenate([high, low, high], 1).astype(BF16)

    def gate_weights(values):
        high, low = split(values)
        return jnp.concatenate([high, high, low], 0).astype(BF16)

    dqgate = by_gate(dqgate_ref[...] + du_pos)
    dxgate = by_gate(jnp.concatenate([dxgate[:, :PARTS_SIZE], du_pos], 0))
    wq = gate_weights(wqt_ref[...])
    wx = gate_weights(wxt_ref[...])

    for p in range(PARTS_SIZE):
        cols = slice(p * PW, (p + 1) * PW)
        q_unit = unit_ref[:, cols]
        dc = dcos_pos[:, p : p + 1]
        p_norm = x_norms[NEG:, p : p + 1]
        p_unit = x_ref[NEG:, cols].astype(F32) * p_norm
        d_unit = matmul(dcosr_ref[p], x_ref[:NEG, cols]) * share + dc * p_unit
        along = jnp.sum(d_unit * q_unit, -1, keepdims=True)
        qgrad_ref[:, cols] = (q_norms[p] * (d_unit - q_unit * along) + matmul(dqgate, wq[:, cols])).astype(BF16)

        gate_term = matmul(dxgate, wx[:, cols])
        dpos_p = p_norm * dc * (q_unit - p_unit * pos_cos[:, p : p + 1]) + gate_term[NEG:]
        dx_ref[NEG:, cols] = dpos_p.astype(BF16)

        x_norm = x_norms[:NEG, p : p + 1]
        x_unit = x_ref[:NEG, cols].astype(F32) * x_norm
        d_unit = matmul_tn(dcos_ref[p], (q_unit * share).astype(BF16))
        along = jnp.sum(d_unit * x_unit, -1, keepdims=True)
        dx_ref[:NEG, cols] = (x_norm * (d_unit - x_unit * along) + gate_term[:NEG]).astype(BF16)

    for part in range(4):
        size = 2 * HALF_ROWS // 4
        row = lax.broadcasted_iota(jnp.int32, (size, NEG + TOK), 0) + part * size
        hot = (back_ref[...] == row).astype(F32).astype(BF16)
        grads_ref[part * size : (part + 1) * size, :] = matmul(hot, dx_ref[...]).astype(BF16)


def loss_and_grads(query, near, far, place, back, w_qgate, w_xgate):
    outs = (
        jax.ShapeDtypeStruct((TOK, 1), F32),
        jax.ShapeDtypeStruct((TOK, D), BF16),
        jax.ShapeDtypeStruct((2 * HALF_ROWS, D), BF16),
    )
    scratch = [
        pltpu.VMEM((NEG + TOK, D), BF16),
        pltpu.VMEM((TOK, D), F32),
        pltpu.VMEM((PARTS_SIZE, TOK, NEG), F32),
        pltpu.VMEM((PARTS_SIZE, TOK, NEG), BF16),
        pltpu.VMEM((PARTS_SIZE, TOK, NEG), BF16),
        pltpu.VMEM((2 * PARTS_SIZE, NEG), F32),
        pltpu.VMEM((TOK, PARTS_SIZE), F32),
        pltpu.VMEM((PARTS_SIZE, 8, NEG), F32),
        pltpu.VMEM((NEG + TOK, D), BF16),
        pltpu.VMEM((PARTS_SIZE, TILE, NEG), F32),
    ]
    return vmem_call(loss_body, outs, scratch=scratch, flops=8 * 10**9, moved=10 * 2**20, name="loss")(
        query, near, far, place.reshape(-1, 1), back, w_qgate.T, w_xgate.T
    )


def local(
    tokens,
    lengths,
    in_gain,
    out_gain,
    w_in,
    w_out,
    w_qgate,
    w_xgate,
    item_table,
    neg_owner,
    neg_slot,
    pos_owner,
    pos_slot,
):
    own_tokens = tokens[0]
    half = lax.axis_index("zh").astype(jnp.int32)[None]
    grp = lax.axis_index("grp").astype(jnp.int32)[None]
    barrier = lax.optimization_barrier

    quarter = lax.dynamic_slice_in_dim(item_table, grp[0] * QUARTER, QUARTER, 0)
    tables = lax.all_gather(quarter, COLUMN, tiled=True)

    gate_query, key_value = front_kernel(own_tokens, in_gain[None], w_in)
    kvs = [key_value]
    for _ in range(2):
        kvs.append(lax.ppermute(kvs[-1], "grp", [(i, i + 1) for i in range(3)]))

    half_then, _ = barrier((half, key_value))
    ask, place, back = pack(
        half_then,
        neg_owner.reshape(1, NEG),
        neg_slot.reshape(1, NEG),
        pos_owner.reshape(1, TOK),
        pos_slot.reshape(1, TOK),
    )
    asked = lax.all_to_all(ask, PLANE, split_axis=0, concat_axis=0, tiled=True)

    asked_then, _ = barrier((asked, key_value))
    near_ids = asked_then[:, :CAP].reshape(-1, 1)
    far_ids = asked_then[:, CAP:].reshape(-1, 1)
    near = lax.all_to_all(look(near_ids, item_table), PLANE, split_axis=0, concat_axis=0, tiled=True)
    far_ids, _ = barrier((far_ids, kvs[1]))
    far_table = lax.dynamic_slice_in_dim(tables, (1 - half[0]) * ITEMS, ITEMS, 0)
    looked = look(far_ids, far_table, 20)
    far = lax.all_to_all(looked, PLANE, split_axis=0, concat_axis=0, tiled=True)

    kvs[2], _ = barrier((kvs[2], looked))
    kvs.append(lax.ppermute(kvs[2], "grp", [(i, i + 1) for i in range(3)]))
    query = attend(grp, lengths, own_tokens, gate_query, kvs, out_gain[None], w_out)

    losses, query_grad, grads = loss_and_grads(query, near, far, place, back, w_qgate, w_xgate)

    came = lax.all_to_all(grads, PLANE, split_axis=0, concat_axis=0, tiled=True)
    shard = half[0] ^ (lax.broadcasted_iota(jnp.int32, asked.shape, 1) // CAP)
    at = half * 4 + grp
    row = (asked + shard * ITEMS - at[0] * QUARTER) & (2 * ITEMS - 1)
    first, *pieces = add_up(at, jnp.where(asked >= 0, row, -1).reshape(1, -1), came)
    first = lax.psum_scatter(first, COLUMN, tiled=True)
    rest = ring_sum(pieces)
    return (losses.reshape(1, TOK), query_grad[None], spread(grp, relay(first) + relay(rest)))


def solution(mesh):
    fine = Mesh(mesh.devices.reshape(4, 4, 2, 4, 2), ("grp", "y", "zh", "x", "core"))
    in_specs = (
        P(SEQ, "grp", None),
        P(SEQ, None),
        P(),
        P(),
        P(),
        P(),
        P(),
        P(),
        P(SEQ, None),
        P(SEQ, "grp", None),
        P(SEQ, "grp"),
        P(SEQ, "grp", None),
        P(SEQ, "grp"),
    )
    out_specs = (P(SEQ, "grp"), P(SEQ, "grp", None), P(SEQ, None))
    return jax.shard_map(local, mesh=fine, in_specs=in_specs, out_specs=out_specs, check_vma=False)
```

```python
import math

import jax
import jax.numpy as jnp
from jax import lax
from jax.experimental import pallas as pl
from jax.experimental.pallas import tpu as pltpu
from jax.sharding import Mesh
from jax.sharding import PartitionSpec as P

HEADS = 4
PARTS_SIZE = 8
INV_TEMP = 32.0
GATE_SCALE = 2.0

D = 1024
TOK = 256
NEG = 512
ITEMS = 512
CAPN = 16
CAPP = 8
CAP = CAPN + CAPP
PEERS = 32
HALF_ROWS = PEERS * CAP
QUARTER = ITEMS // 4
WIDTHS = (512, 512)
ATTEND_COST = 8 * 10**9
QKW = 256
PW = D // PARTS_SIZE
TILE = 16

PLANE = ("y", "x", "core")
SEQ = ("y", "zh", "x", "core")
COLUMN = ("zh", "grp")

F32 = jnp.float32
BF16 = jnp.bfloat16
HIGHEST = lax.Precision.HIGHEST


def matmul(a, b):
    return jnp.dot(a, b, preferred_element_type=F32)


def matmul_nt(a, b, precision=None):
    return lax.dot_general(a, b, (((1,), (1,)), ((), ())), precision=precision, preferred_element_type=F32)


def matmul_tn(a, b, precision=None):
    return lax.dot_general(a, b, (((0,), (0,)), ((), ())), precision=precision, preferred_element_type=F32)


def vmem_call(body, outs, n_smem=0, n_any=0, scratch=(), limit=50, flops=0, moved=0, name=None):
    def call(*args):
        in_specs = [pl.BlockSpec(memory_space=pltpu.SMEM)] * n_smem
        in_specs += [pl.BlockSpec(memory_space=pl.ANY)] * n_any
        in_specs += [pl.BlockSpec(memory_space=pltpu.VMEM)] * (len(args) - n_smem - n_any)
        return pl.pallas_call(
            body,
            out_shape=outs,
            in_specs=in_specs,
            out_specs=jax.tree.map(lambda _: pl.BlockSpec(memory_space=pltpu.VMEM), outs),
            scratch_shapes=list(scratch),
            compiler_params=pltpu.CompilerParams(vmem_limit_bytes=limit * 2**20),
            cost_estimate=pl.CostEstimate(flops=flops, bytes_accessed=moved, transcendentals=0),
            name=name,
        )(*args)

    return call


def pack_body(half_ref, nown_ref, nslot_ref, pown_ref, pslot_ref, ask_ref, place_ref, back_ref, owner_ref, slot_ref, sems):
    total = NEG + TOK
    pairs = (
        (nown_ref, owner_ref.at[:, :NEG]),
        (nslot_ref, slot_ref.at[:, :NEG]),
        (pown_ref, owner_ref.at[:, NEG:]),
        (pslot_ref, slot_ref.at[:, NEG:]),
    )
    copies = [pltpu.make_async_copy(a, b, sems.at[i]) for i, (a, b) in enumerate(pairs)]
    for copy in copies:
        copy.start()
    for copy in copies:
        copy.wait()
    owner = owner_ref[...]
    slot = slot_ref[...]
    lane = lax.broadcasted_iota(jnp.int32, (1, total), 1)
    positive = (lane >= NEG).astype(jnp.int32)
    far = ((owner >> 3) & 1) ^ half_ref[0]
    peer = (owner >> 4) * 8 + (owner & 7)
    key = positive * 64 + far * 32 + peer
    hot = key == lax.broadcasted_iota(jnp.int32, (128, total), 0)
    before = lax.broadcasted_iota(jnp.int32, (total, total), 0) < lax.broadcasted_iota(jnp.int32, (total, total), 1)
    counts = matmul(hot.astype(F32).astype(BF16), before.astype(F32).astype(BF16))
    rank = jnp.sum(jnp.where(hot, counts, 0.0), 0, keepdims=True).astype(jnp.int32)
    inner = rank + positive * CAPN
    column = far * CAP + inner
    peer_hot = (peer == lax.broadcasted_iota(jnp.int32, (PEERS, total), 0)).astype(F32).astype(BF16)
    here = column == lax.broadcasted_iota(jnp.int32, (2 * CAP, total), 0)
    value = slot + 1
    high = jnp.where(here, (value >> 5).astype(F32), 0.0).astype(BF16)
    low = jnp.where(here, (value & 31).astype(F32), 0.0).astype(BF16)
    ids = matmul_nt(peer_hot, high) * 32.0 + matmul_nt(peer_hot, low)
    ask_ref[...] = ids.astype(jnp.int32) - 1
    place_ref[...] = far * HALF_ROWS + peer * CAP + inner
    back_ref[...] = peer * (2 * CAP) + column


def pack(half, neg_owner, neg_slot, pos_owner, pos_slot):
    outs = (
        jax.ShapeDtypeStruct((PEERS, 2 * CAP), jnp.int32),
        jax.ShapeDtypeStruct((1, NEG + TOK), jnp.int32),
        jax.ShapeDtypeStruct((1, NEG + TOK), jnp.int32),
    )
    row = pltpu.VMEM((1, NEG + TOK), jnp.int32)
    return vmem_call(
        pack_body, outs, n_smem=1, n_any=4, scratch=[row, row, pltpu.SemaphoreType.DMA((4,))], name="pack"
    )(half, neg_owner, neg_slot, pos_owner, pos_slot)


def look_body(ids_ref, table_ref, rows_ref):
    hot = ids_ref[...] == lax.broadcasted_iota(jnp.int32, (HALF_ROWS, ITEMS), 1)
    rows_ref[...] = matmul(hot.astype(F32).astype(BF16), table_ref[...]).astype(BF16)


def look(ids, table, cost=1):
    outs = jax.ShapeDtypeStruct((HALF_ROWS, D), BF16)
    return vmem_call(look_body, outs, flops=cost * 2 * HALF_ROWS * ITEMS * D, moved=4 * 2**20, name="look")(ids, table)


def relay(own):
    moved = [lax.ppermute(own, "grp", [(i, (i + k) % 4) for i in range(4)]) for k in (1, 2, 3)]
    return [own] + moved


def lay_out(grp, refs, out_ref, cols):
    for k, ref in enumerate(refs):
        at = ((grp - k) & 3) * QUARTER
        out_ref[pl.ds(pl.multiple_of(at, QUARTER), QUARTER), cols] = ref[...].astype(out_ref.dtype)


def spread_body(grp_ref, *refs):
    out_ref = refs[-1]
    at = 0
    for i, width in enumerate(WIDTHS):
        lay_out(grp_ref[0], refs[4 * i : 4 * i + 4], out_ref, slice(at, at + width))
        at += width


def spread(grp, quarters):
    outs = jax.ShapeDtypeStruct((ITEMS, D), F32)
    return vmem_call(spread_body, outs, n_smem=1, moved=3 * 2**20, name="spread")(grp, *quarters)


def column_hop(value, step, senders):
    place = [(i % 4) * 2 + i // 4 for i in range(8)]
    pairs = [(place[i], place[(i + step) % 8]) for i in range(8) if i % 4 in senders]
    return lax.ppermute(value, ("grp", "zh"), pairs)


def look_far_body(grp_ref, ids_ref, q0, q1, q2, q3, rows_ref, table_ref):
    lay_out(grp_ref[0], (q0, q1, q2, q3), table_ref, slice(0, D))
    look_body(ids_ref, table_ref, rows_ref)


def look_far(grp, ids, quarters, cost):
    outs = jax.ShapeDtypeStruct((HALF_ROWS, D), BF16)
    return vmem_call(
        look_far_body, outs, n_smem=1, scratch=[pltpu.VMEM((ITEMS, D), BF16)], flops=cost * 2 * HALF_ROWS * ITEMS * D,
        moved=4 * 2**20, name="look_far",
    )(grp, ids, *quarters)


def add_body(ids_ref, grads_ref, *piece_refs):
    eighth = 2 * ITEMS // 8
    for pair in range(4):
        row = lax.broadcasted_iota(jnp.int32, (2 * eighth, 2 * HALF_ROWS), 0) + pair * 2 * eighth
        hot = (ids_ref[...] == row).astype(F32).astype(BF16)
        summed = matmul(hot, grads_ref[...]).astype(BF16)
        for i in range(2):
            at = 0
            for part, width in enumerate(WIDTHS):
                ref = piece_refs[8 * part + 2 * pair + i]
                ref[...] = summed[i * eighth : (i + 1) * eighth, at : at + width]
                at += width


def add_up(ids, grads):
    outs = sum(((jax.ShapeDtypeStruct((ITEMS // 4, width), BF16),) * 8 for width in WIDTHS), ())
    return vmem_call(add_body, outs, flops=8 * HALF_ROWS * ITEMS * D, moved=5 * 2**20, name="add_up")(ids, grads)


def ring_sum(pieces):
    def hop(value, step):
        return column_hop(value, step, range(4))

    def plus(value, piece):
        return (value.astype(F32) + piece.astype(F32)).astype(BF16)

    back = hop(pieces[4], -1)
    ahead = hop(pieces[3], 1)
    back = hop(plus(back, pieces[5]), -1)
    ahead = hop(plus(ahead, pieces[2]), 1)
    back = hop(plus(back, pieces[6]), -1)
    ahead = hop(plus(ahead, pieces[1]), 1)
    back = hop(plus(back, pieces[7]), -1)
    return (pieces[0].astype(F32) + back.astype(F32) + ahead.astype(F32)).astype(BF16)


def layer_norm(values, gain_vec):
    average = jnp.mean(values, -1, keepdims=True)
    centred = values - average
    spread = jnp.mean(centred * centred, -1, keepdims=True)
    return centred * lax.rsqrt(spread + 1e-05) * gain_vec


def front_body(tok_ref, gain_ref, w_ref, gq_ref, kv_ref):
    normed = layer_norm(tok_ref[...].astype(F32), gain_ref[...]).astype(BF16)

    def project(first, size):
        half = 0.5 * matmul(normed, w_ref[:, first : first + size])
        return (half + half * jnp.tanh(half)).astype(BF16)

    for at in range(0, D, 512):
        kv_ref[:, at : at + 512] = project(D + at, 512)
    kv_ref[:, D:] = project(2 * D + QKW, QKW)
    for at in range(0, D, 512):
        gq_ref[:, at : at + 512] = project(at, 512)
    gq_ref[:, D:] = project(2 * D, QKW)


def front_kernel(own_tokens, in_gain, w_in):
    out = jax.ShapeDtypeStruct((TOK, D + QKW), BF16)
    return vmem_call(front_body, (out, out), flops=14 * 10**8, moved=7 * 2**20, name="front")(own_tokens, in_gain, w_in)


def attend_blocks(grp_ref, len_ref, gq_ref, kv_refs, first):
    start = grp_ref[0] * TOK
    ends = [len_ref[0, 0]]
    for i in range(1, len_ref.shape[1]):
        ends.append(ends[-1] + len_ref[0, i])

    def segment(pos):
        return sum((pos >= end).astype(jnp.int32) for end in ends)

    query_pos = start + lax.broadcasted_iota(jnp.int32, (TOK, 1), 0)
    query_seg = segment(query_pos)
    masks = []
    for hop in range(first, first + len(kv_refs)):
        key_pos = start - hop * TOK + lax.broadcasted_iota(jnp.int32, (1, TOK), 1)
        seen = (query_seg == segment(key_pos)) & (key_pos >= 0) & (key_pos <= query_pos)
        masks.append(jnp.where(seen, 0.5 / math.sqrt(QKW // HEADS), 0.0))
    qkh = QKW // HEADS
    vh = D // HEADS
    for head in range(HEADS):
        query = gq_ref[:, D + head * qkh : D + (head + 1) * qkh]
        acc = jnp.zeros((TOK, vh), F32)
        for mask, ref in zip(masks, kv_refs):
            key = ref[:, D + head * qkh : D + (head + 1) * qkh]
            value = ref[:, head * vh : (head + 1) * vh]
            scores = matmul_nt(query, key) * mask
            weights = (scores + scores * jnp.tanh(scores)).astype(BF16)
            acc = acc + matmul(weights, value)
        yield slice(head * vh, (head + 1) * vh), acc


def near_body(grp_ref, len_ref, gq_ref, kv0_ref, kv1_ref, kv2_ref, mixed_ref):
    for cols, acc in attend_blocks(grp_ref, len_ref, gq_ref, (kv0_ref, kv1_ref, kv2_ref), 0):
        mixed_ref[:, cols] = acc


def last_body(grp_ref, len_ref, tok_ref, gq_ref, part_ref, kv3_ref, gain_ref, wout_ref, out_ref, mixed_ref):
    for cols, acc in attend_blocks(grp_ref, len_ref, gq_ref, (kv3_ref,), 3):
        mixed_ref[:, cols] = part_ref[:, cols] + acc
    gated = (layer_norm(mixed_ref[...], gain_ref[...]) * gq_ref[:, :D].astype(F32)).astype(BF16)
    out_ref[...] = tok_ref[...].astype(F32) + matmul(gated, wout_ref[...])


def attend(grp, lengths, own_tokens, gq, kvs, out_gain, w_out):
    outs = jax.ShapeDtypeStruct((TOK, D), F32)
    part = vmem_call(near_body, outs, n_smem=2, flops=10**9, moved=4 * 2**20, name="attend_near")(
        grp, lengths, gq, *kvs[:3]
    )
    return vmem_call(
        last_body, outs, n_smem=2, scratch=[pltpu.VMEM((TOK, D), F32)], flops=ATTEND_COST, moved=8 * 2**20, name="attend_last"
    )(grp, lengths, own_tokens, gq, part, kvs[3], out_gain, w_out)


def gate_of(u):
    t = jnp.tanh(u)
    return t, jnp.exp(GATE_SCALE * t)


def split(values):
    high = values.astype(BF16).astype(F32)
    return high, values - high


def split_rows(values):
    high, rest = split(values)
    middle, low = split(rest)
    return jnp.concatenate([high, middle, low], 0).astype(BF16)


def loss_body(
    query_ref, near_ref, far_ref, place_ref, back_ref, wqt_ref, wxt_ref,
    loss_ref, qgrad_ref, grads_ref,
    x_ref, unit_ref, cos_ref, dcos_ref, dcosr_ref, side_ref, dqgate_ref, dxgate_ref, dx_ref, du_ref,
):
    lanes = lax.broadcasted_iota(jnp.int32, (NEG + TOK, HALF_ROWS), 1)
    hot_near = (place_ref[...] == lanes).astype(F32).astype(BF16)
    hot_far = (place_ref[...] == lanes + HALF_ROWS).astype(F32).astype(BF16)
    x_ref[...] = (matmul(hot_near, near_ref[...]) + matmul(hot_far, far_ref[...])).astype(BF16)

    part_of = lax.broadcasted_iota(jnp.int32, (16, D), 1) // PW
    pick = (part_of == lax.broadcasted_iota(jnp.int32, (16, D), 0)).astype(F32).astype(BF16)
    eye = lax.broadcasted_iota(jnp.int32, (1, PARTS_SIZE), 1)

    rows = x_ref[...].astype(F32)
    high, low = split(rows * rows)
    squares = matmul_nt(high.astype(BF16), pick) + matmul_nt(low.astype(BF16), pick)
    x_norms = lax.rsqrt(squares[:, :PARTS_SIZE] + 1e-06)
    terms = matmul_nt(x_ref[...], split_rows(wxt_ref[...]))
    xgate = terms[:, :8] + terms[:, 8:16] + terms[:, 16:]
    side = jnp.concatenate([xgate[:NEG], x_norms[:NEG], jnp.zeros((NEG, 112), F32)], 1)
    side_ref[...] = jnp.transpose(side)[:16, :]
    pgate = xgate[NEG:]

    query = query_ref[...]
    qgate = matmul_nt(query, wqt_ref[...], HIGHEST)

    pos_cos = jnp.zeros((TOK, PARTS_SIZE), F32)
    q_norms = []
    for p in range(PARTS_SIZE):
        cols = slice(p * PW, (p + 1) * PW)
        q_p = query_ref[:, cols]
        q_norm = lax.rsqrt(jnp.sum(q_p * q_p, -1, keepdims=True) + 1e-06)
        q_unit = q_p * q_norm
        unit_ref[:, cols] = q_unit
        q_high, q_low = split(q_unit)
        x_p = x_ref[:NEG, cols]
        q_two = jnp.concatenate([q_high.astype(BF16), q_low.astype(BF16)], 1)
        cos_ref[p] = matmul_nt(q_two, jnp.concatenate([x_p, x_p], 1)) * side_ref[8 + p : 9 + p, :]
        dot_p = jnp.sum(q_unit * x_ref[NEG:, cols].astype(F32), -1, keepdims=True)
        pos_cos = jnp.where(eye == p, dot_p, pos_cos)
        q_norms.append(q_norm)
    pos_cos = pos_cos * x_norms[NEG:]

    t_pos, e_pos = gate_of(qgate + pgate)
    mix_pos = e_pos / jnp.sum(e_pos, -1, keepdims=True)
    mean_pos = jnp.sum(mix_pos * pos_cos, -1, keepdims=True)
    pos_logit = INV_TEMP * mean_pos
    raised_pos = jnp.exp(pos_logit)

    dxgate_ref[...] = jnp.zeros_like(dxgate_ref)
    dqgate_ref[...] = qgate
    loss_ref[...] = raised_pos

    def tile(i, carry):
        rows = pl.ds(pl.multiple_of(i * TILE, TILE), TILE)
        qg = dqgate_ref[rows, :]
        qgs = [jnp.broadcast_to(qg[:, p : p + 1], (TILE, PW)) for p in range(PARTS_SIZE)]
        sums = [jnp.zeros((TILE, PW), F32) for _ in range(PARTS_SIZE)]
        part = jnp.zeros((TILE, PW), F32)
        for block in range(NEG // PW):
            cols = slice(block * PW, (block + 1) * PW)
            ts, es, cs = [], [], []
            total = jnp.zeros((TILE, PW), F32)
            mixed = jnp.zeros((TILE, PW), F32)
            for p in range(PARTS_SIZE):
                t, e = gate_of(qgs[p] + side_ref[p : p + 1, cols])
                c = cos_ref[p, rows, cols]
                total = total + e
                mixed = mixed + e * c
                ts.append(t)
                es.append(e)
                cs.append(c)
            inverse = 1.0 / total
            mean = mixed * inverse
            raised = jnp.exp(INV_TEMP * mean)
            part = part + raised
            scaled = raised * inverse
            for p in range(PARTS_SIZE):
                dcos = scaled * es[p]
                du = dcos * (cs[p] - mean) * (1.0 - ts[p] * ts[p])
                dcos_ref[p, rows, cols] = dcos.astype(BF16)
                dcosr_ref[p, rows, cols] = (dcos * side_ref[8 + p : 9 + p, cols]).astype(BF16)
                du_ref[p, :, cols] = du
                sums[p] = sums[p] + du
        partition = loss_ref[rows, :] + jnp.sum(part, -1, keepdims=True)
        factor = (GATE_SCALE * INV_TEMP) / partition
        dq = jnp.zeros((TILE, PARTS_SIZE), F32)
        for p in range(PARTS_SIZE):
            du = du_ref[p] * factor
            dxgate_ref[p] += du[:8] + du[8:]
            dq = jnp.where(eye == p, jnp.sum(sums[p], -1, keepdims=True), dq)
        dqgate_ref[rows, :] = dq * factor
        loss_ref[rows, :] = partition
        return carry

    lax.fori_loop(0, TOK // TILE, tile, 0, unroll=2)

    partition = loss_ref[...]
    loss_ref[...] = jnp.log(partition) - pos_logit
    share = INV_TEMP / partition
    dpos = INV_TEMP * (raised_pos / partition - 1.0)
    dcos_pos = dpos * mix_pos
    du_pos = dcos_pos * (pos_cos - mean_pos) * (GATE_SCALE - GATE_SCALE * t_pos * t_pos)
    dxgate = jnp.transpose(jnp.concatenate([jnp.sum(dxgate_ref[...], 1), jnp.zeros((120, NEG), F32)], 0))

    def by_gate(values):
        high, low = split(values)
        return jnp.concatenate([high, low, high], 1).astype(BF16)

    def gate_weights(values):
        high, low = split(values)
        return jnp.concatenate([high, high, low], 0).astype(BF16)

    dqgate = by_gate(dqgate_ref[...] + du_pos)
    dxgate = by_gate(jnp.concatenate([dxgate[:, :PARTS_SIZE], du_pos], 0))
    wq = gate_weights(wqt_ref[...])
    wx = gate_weights(wxt_ref[...])

    for p in range(PARTS_SIZE):
        cols = slice(p * PW, (p + 1) * PW)
        q_unit = unit_ref[:, cols]
        dc = dcos_pos[:, p : p + 1]
        p_norm = x_norms[NEG:, p : p + 1]
        p_unit = x_ref[NEG:, cols].astype(F32) * p_norm
        d_unit = matmul(dcosr_ref[p], x_ref[:NEG, cols]) * share + dc * p_unit
        along = jnp.sum(d_unit * q_unit, -1, keepdims=True)
        qgrad_ref[:, cols] = (q_norms[p] * (d_unit - q_unit * along) + matmul(dqgate, wq[:, cols])).astype(BF16)

        gate_term = matmul(dxgate, wx[:, cols])
        dpos_p = p_norm * dc * (q_unit - p_unit * pos_cos[:, p : p + 1]) + gate_term[NEG:]
        dx_ref[NEG:, cols] = dpos_p.astype(BF16)

        x_norm = x_norms[:NEG, p : p + 1]
        x_unit = x_ref[:NEG, cols].astype(F32) * x_norm
        d_unit = matmul_tn(dcos_ref[p], (q_unit * share).astype(BF16))
        along = jnp.sum(d_unit * x_unit, -1, keepdims=True)
        dx_ref[:NEG, cols] = (x_norm * (d_unit - x_unit * along) + gate_term[:NEG]).astype(BF16)

    for part in range(4):
        size = 2 * HALF_ROWS // 4
        row = lax.broadcasted_iota(jnp.int32, (size, NEG + TOK), 0) + part * size
        hot = (back_ref[...] == row).astype(F32).astype(BF16)
        grads_ref[part * size : (part + 1) * size, :] = matmul(hot, dx_ref[...]).astype(BF16)


def loss_and_grads(query, near, far, place, back, w_qgate, w_xgate):
    outs = (
        jax.ShapeDtypeStruct((TOK, 1), F32),
        jax.ShapeDtypeStruct((TOK, D), BF16),
        jax.ShapeDtypeStruct((2 * HALF_ROWS, D), BF16),
    )
    scratch = [
        pltpu.VMEM((NEG + TOK, D), BF16),
        pltpu.VMEM((TOK, D), F32),
        pltpu.VMEM((PARTS_SIZE, TOK, NEG), F32),
        pltpu.VMEM((PARTS_SIZE, TOK, NEG), BF16),
        pltpu.VMEM((PARTS_SIZE, TOK, NEG), BF16),
        pltpu.VMEM((2 * PARTS_SIZE, NEG), F32),
        pltpu.VMEM((TOK, PARTS_SIZE), F32),
        pltpu.VMEM((PARTS_SIZE, 8, NEG), F32),
        pltpu.VMEM((NEG + TOK, D), BF16),
        pltpu.VMEM((PARTS_SIZE, TILE, NEG), F32),
    ]
    return vmem_call(loss_body, outs, scratch=scratch, flops=8 * 10**9, moved=10 * 2**20, name="loss")(
        query, near, far, place.reshape(-1, 1), back, w_qgate.T, w_xgate.T
    )


def local(
    tokens,
    lengths,
    in_gain,
    out_gain,
    w_in,
    w_out,
    w_qgate,
    w_xgate,
    item_table,
    neg_owner,
    neg_slot,
    pos_owner,
    pos_slot,
):
    own_tokens = tokens[0]
    half = lax.axis_index("zh").astype(jnp.int32)[None]
    grp = lax.axis_index("grp").astype(jnp.int32)[None]
    barrier = lax.optimization_barrier

    gate_query, key_value = front_kernel(own_tokens, in_gain[None], w_in)
    kvs = [key_value]
    for _ in range(2):
        kvs.append(lax.ppermute(kvs[-1], "grp", [(i, i + 1) for i in range(3)]))

    grp_then, _ = barrier((grp, key_value))
    quarter = lax.dynamic_slice_in_dim(item_table, grp_then[0] * QUARTER, QUARTER, 0)
    moved = lax.ppermute(quarter, "zh", [(0, 1), (1, 0)])

    half_then, _ = barrier((half, quarter))
    ask, place, back = pack(
        half_then,
        neg_owner.reshape(1, NEG),
        neg_slot.reshape(1, NEG),
        pos_owner.reshape(1, TOK),
        pos_slot.reshape(1, TOK),
    )
    asked = lax.all_to_all(ask, PLANE, split_axis=0, concat_axis=0, tiled=True)

    moved_then, _ = barrier((moved, ask))
    arrivals = relay(moved_then)

    asked_then, _ = barrier((asked, kvs[1]))
    near_ids = asked_then[:, :CAP].reshape(-1, 1)
    far_ids = asked_then[:, CAP:].reshape(-1, 1)
    looked = look(near_ids, item_table)
    near = lax.all_to_all(looked, PLANE, split_axis=0, concat_axis=0, tiled=True)

    far_ids, _ = barrier((far_ids, looked))
    looked = look_far(grp, far_ids, arrivals, 20)
    far = lax.all_to_all(looked, PLANE, split_axis=0, concat_axis=0, tiled=True)

    kvs[2], _ = barrier((kvs[2], looked))
    kvs.append(lax.ppermute(kvs[2], "grp", [(i, i + 1) for i in range(3)]))
    query = attend(grp, lengths, own_tokens, gate_query, kvs, out_gain[None], w_out)

    losses, query_grad, grads = loss_and_grads(query, near, far, place, back, w_qgate, w_xgate)

    came = lax.all_to_all(grads, PLANE, split_axis=0, concat_axis=0, tiled=True)
    shard = half[0] ^ (lax.broadcasted_iota(jnp.int32, asked.shape, 1) // CAP)
    row = (asked + shard * ITEMS - (half[0] * 4 + grp[0]) * QUARTER) & (2 * ITEMS - 1)
    pieces = add_up(jnp.where(asked >= 0, row, -1).reshape(1, -1), came)
    sums = [ring_sum(pieces[8 * part : 8 * part + 8]) for part in range(len(WIDTHS))]
    return (losses.reshape(1, TOK), query_grad[None], spread(grp, sum((relay(part) for part in sums), [])))


def solution(mesh):
    fine = Mesh(mesh.devices.reshape(4, 4, 2, 4, 2), ("grp", "y", "zh", "x", "core"))
    in_specs = (
        P(SEQ, "grp", None),
        P(SEQ, None),
        P(),
        P(),
        P(),
        P(),
        P(),
        P(),
        P(SEQ, None),
        P(SEQ, "grp", None),
        P(SEQ, "grp"),
        P(SEQ, "grp", None),
        P(SEQ, "grp"),
    )
    out_specs = (P(SEQ, "grp"), P(SEQ, "grp", None), P(SEQ, None))
    return jax.shard_map(local, mesh=fine, in_specs=in_specs, out_specs=out_specs, check_vma=False)
```

```python
import math

import jax
import jax.numpy as jnp
from jax import lax
from jax.experimental import pallas as pl
from jax.experimental.pallas import tpu as pltpu
from jax.sharding import Mesh
from jax.sharding import PartitionSpec as P

HEADS = 4
PARTS_SIZE = 8
INV_TEMP = 32.0
GATE_SCALE = 2.0

D = 1024
TOK = 256
NEG = 512
ITEMS = 512
CAPN = 16
CAPP = 8
CAP = CAPN + CAPP
PEERS = 32
HALF_ROWS = PEERS * CAP
QUARTER = ITEMS // 4
WIDTHS = (512, 512)
ATTEND_COST = 8 * 10**9
QKW = 256
PW = D // PARTS_SIZE
TILE = 16

PLANE = ("y", "x", "core")
SEQ = ("y", "zh", "x", "core")
COLUMN = ("zh", "grp")

F32 = jnp.float32
BF16 = jnp.bfloat16
HIGHEST = lax.Precision.HIGHEST


def matmul(a, b):
    return jnp.dot(a, b, preferred_element_type=F32)


def matmul_nt(a, b, precision=None):
    return lax.dot_general(a, b, (((1,), (1,)), ((), ())), precision=precision, preferred_element_type=F32)


def matmul_tn(a, b, precision=None):
    return lax.dot_general(a, b, (((0,), (0,)), ((), ())), precision=precision, preferred_element_type=F32)


def vmem_call(body, outs, n_smem=0, n_any=0, scratch=(), limit=50, flops=0, moved=0, name=None):
    def call(*args):
        in_specs = [pl.BlockSpec(memory_space=pltpu.SMEM)] * n_smem
        in_specs += [pl.BlockSpec(memory_space=pl.ANY)] * n_any
        in_specs += [pl.BlockSpec(memory_space=pltpu.VMEM)] * (len(args) - n_smem - n_any)
        return pl.pallas_call(
            body,
            out_shape=outs,
            in_specs=in_specs,
            out_specs=jax.tree.map(lambda _: pl.BlockSpec(memory_space=pltpu.VMEM), outs),
            scratch_shapes=list(scratch),
            compiler_params=pltpu.CompilerParams(vmem_limit_bytes=limit * 2**20),
            cost_estimate=pl.CostEstimate(flops=flops, bytes_accessed=moved, transcendentals=0),
            name=name,
        )(*args)

    return call


def pack_body(half_ref, nown_ref, nslot_ref, pown_ref, pslot_ref, ask_ref, place_ref, back_ref, owner_ref, slot_ref, sems):
    total = NEG + TOK
    pairs = (
        (nown_ref, owner_ref.at[:, :NEG]),
        (nslot_ref, slot_ref.at[:, :NEG]),
        (pown_ref, owner_ref.at[:, NEG:]),
        (pslot_ref, slot_ref.at[:, NEG:]),
    )
    copies = [pltpu.make_async_copy(a, b, sems.at[i]) for i, (a, b) in enumerate(pairs)]
    for copy in copies:
        copy.start()
    for copy in copies:
        copy.wait()
    owner = owner_ref[...]
    slot = slot_ref[...]
    lane = lax.broadcasted_iota(jnp.int32, (1, total), 1)
    positive = (lane >= NEG).astype(jnp.int32)
    far = ((owner >> 3) & 1) ^ half_ref[0]
    peer = (owner >> 4) * 8 + (owner & 7)
    key = positive * 64 + far * 32 + peer
    hot = key == lax.broadcasted_iota(jnp.int32, (128, total), 0)
    before = lax.broadcasted_iota(jnp.int32, (total, total), 0) < lax.broadcasted_iota(jnp.int32, (total, total), 1)
    counts = matmul(hot.astype(F32).astype(BF16), before.astype(F32).astype(BF16))
    rank = jnp.sum(jnp.where(hot, counts, 0.0), 0, keepdims=True).astype(jnp.int32)
    inner = rank + positive * CAPN
    column = far * CAP + inner
    peer_hot = (peer == lax.broadcasted_iota(jnp.int32, (PEERS, total), 0)).astype(F32).astype(BF16)
    here = column == lax.broadcasted_iota(jnp.int32, (2 * CAP, total), 0)
    value = slot + 1
    high = jnp.where(here, (value >> 5).astype(F32), 0.0).astype(BF16)
    low = jnp.where(here, (value & 31).astype(F32), 0.0).astype(BF16)
    ids = matmul_nt(peer_hot, high) * 32.0 + matmul_nt(peer_hot, low)
    ask_ref[...] = ids.astype(jnp.int32) - 1
    place_ref[...] = far * HALF_ROWS + peer * CAP + inner
    back_ref[...] = peer * (2 * CAP) + column


def pack(half, neg_owner, neg_slot, pos_owner, pos_slot):
    outs = (
        jax.ShapeDtypeStruct((PEERS, 2 * CAP), jnp.int32),
        jax.ShapeDtypeStruct((1, NEG + TOK), jnp.int32),
        jax.ShapeDtypeStruct((1, NEG + TOK), jnp.int32),
    )
    row = pltpu.VMEM((1, NEG + TOK), jnp.int32)
    return vmem_call(
        pack_body, outs, n_smem=1, n_any=4, scratch=[row, row, pltpu.SemaphoreType.DMA((4,))], name="pack"
    )(half, neg_owner, neg_slot, pos_owner, pos_slot)


def look_body(ids_ref, table_ref, rows_ref):
    hot = ids_ref[...] == lax.broadcasted_iota(jnp.int32, (HALF_ROWS, ITEMS), 1)
    rows_ref[...] = matmul(hot.astype(F32).astype(BF16), table_ref[...]).astype(BF16)


def look(ids, table, cost=1):
    outs = jax.ShapeDtypeStruct((HALF_ROWS, D), BF16)
    return vmem_call(look_body, outs, flops=cost * 2 * HALF_ROWS * ITEMS * D, moved=4 * 2**20, name="look")(ids, table)


def relay(own):
    moved = [lax.ppermute(own, "grp", [(i, (i + k) % 4) for i in range(4)]) for k in (1, 2, 3)]
    return [own] + moved


def lay_out(grp, refs, out_ref, cols):
    for k, ref in enumerate(refs):
        at = ((grp - k) & 3) * QUARTER
        out_ref[pl.ds(pl.multiple_of(at, QUARTER), QUARTER), cols] = ref[...].astype(out_ref.dtype)


def spread_body(grp_ref, *refs):
    out_ref = refs[-1]
    at = 0
    for i, width in enumerate(WIDTHS):
        lay_out(grp_ref[0], refs[4 * i : 4 * i + 4], out_ref, slice(at, at + width))
        at += width


def spread(grp, quarters):
    outs = jax.ShapeDtypeStruct((ITEMS, D), F32)
    return vmem_call(spread_body, outs, n_smem=1, moved=3 * 2**20, name="spread")(grp, *quarters)


def column_hop(value, step, senders):
    place = [(i % 4) * 2 + i // 4 for i in range(8)]
    pairs = [(place[i], place[(i + step) % 8]) for i in range(8) if i % 4 in senders]
    return lax.ppermute(value, ("grp", "zh"), pairs)


def add_body(ids_ref, grads_ref, *piece_refs):
    eighth = 2 * ITEMS // 8
    for pair in range(4):
        row = lax.broadcasted_iota(jnp.int32, (2 * eighth, 2 * HALF_ROWS), 0) + pair * 2 * eighth
        hot = (ids_ref[...] == row).astype(F32).astype(BF16)
        summed = matmul(hot, grads_ref[...]).astype(BF16)
        for i in range(2):
            at = 0
            for part, width in enumerate(WIDTHS):
                ref = piece_refs[8 * part + 2 * pair + i]
                ref[...] = summed[i * eighth : (i + 1) * eighth, at : at + width]
                at += width


def add_up(ids, grads):
    outs = sum(((jax.ShapeDtypeStruct((ITEMS // 4, width), BF16),) * 8 for width in WIDTHS), ())
    return vmem_call(add_body, outs, flops=8 * HALF_ROWS * ITEMS * D, moved=5 * 2**20, name="add_up")(ids, grads)


def ring_sum(pieces):
    def hop(value, step):
        return column_hop(value, step, range(4))

    def plus(value, piece):
        return (value.astype(F32) + piece.astype(F32)).astype(BF16)

    back = hop(pieces[4], -1)
    ahead = hop(pieces[3], 1)
    back = hop(plus(back, pieces[5]), -1)
    ahead = hop(plus(ahead, pieces[2]), 1)
    back = hop(plus(back, pieces[6]), -1)
    ahead = hop(plus(ahead, pieces[1]), 1)
    back = hop(plus(back, pieces[7]), -1)
    return (pieces[0].astype(F32) + back.astype(F32) + ahead.astype(F32)).astype(BF16)


def layer_norm(values, gain_vec):
    average = jnp.mean(values, -1, keepdims=True)
    centred = values - average
    spread = jnp.mean(centred * centred, -1, keepdims=True)
    return centred * lax.rsqrt(spread + 1e-05) * gain_vec


def front_body(tok_ref, gain_ref, w_ref, gq_ref, kv_ref):
    normed = layer_norm(tok_ref[...].astype(F32), gain_ref[...]).astype(BF16)

    def project(first, size):
        half = 0.5 * matmul(normed, w_ref[:, first : first + size])
        return (half + half * jnp.tanh(half)).astype(BF16)

    for at in range(0, D, 512):
        kv_ref[:, at : at + 512] = project(D + at, 512)
    kv_ref[:, D:] = project(2 * D + QKW, QKW)
    for at in range(0, D, 512):
        gq_ref[:, at : at + 512] = project(at, 512)
    gq_ref[:, D:] = project(2 * D, QKW)


def front_kernel(own_tokens, in_gain, w_in):
    out = jax.ShapeDtypeStruct((TOK, D + QKW), BF16)
    return vmem_call(front_body, (out, out), flops=14 * 10**8, moved=7 * 2**20, name="front")(own_tokens, in_gain, w_in)


def attend_blocks(grp_ref, len_ref, gq_ref, kv_refs, first):
    start = grp_ref[0] * TOK
    ends = [len_ref[0, 0]]
    for i in range(1, len_ref.shape[1]):
        ends.append(ends[-1] + len_ref[0, i])

    def segment(pos):
        return sum((pos >= end).astype(jnp.int32) for end in ends)

    query_pos = start + lax.broadcasted_iota(jnp.int32, (TOK, 1), 0)
    query_seg = segment(query_pos)
    masks = []
    for hop in range(first, first + len(kv_refs)):
        key_pos = start - hop * TOK + lax.broadcasted_iota(jnp.int32, (1, TOK), 1)
        seen = (query_seg == segment(key_pos)) & (key_pos >= 0) & (key_pos <= query_pos)
        masks.append(jnp.where(seen, 0.5 / math.sqrt(QKW // HEADS), 0.0))
    qkh = QKW // HEADS
    vh = D // HEADS
    for head in range(HEADS):
        query = gq_ref[:, D + head * qkh : D + (head + 1) * qkh]
        acc = jnp.zeros((TOK, vh), F32)
        for mask, ref in zip(masks, kv_refs):
            key = ref[:, D + head * qkh : D + (head + 1) * qkh]
            value = ref[:, head * vh : (head + 1) * vh]
            scores = matmul_nt(query, key) * mask
            weights = (scores + scores * jnp.tanh(scores)).astype(BF16)
            acc = acc + matmul(weights, value)
        yield slice(head * vh, (head + 1) * vh), acc


def near_body(grp_ref, len_ref, gq_ref, kv0_ref, kv1_ref, kv2_ref, mixed_ref):
    for cols, acc in attend_blocks(grp_ref, len_ref, gq_ref, (kv0_ref, kv1_ref, kv2_ref), 0):
        mixed_ref[:, cols] = acc


def last_body(grp_ref, len_ref, tok_ref, gq_ref, part_ref, kv3_ref, gain_ref, wout_ref, out_ref, mixed_ref):
    for cols, acc in attend_blocks(grp_ref, len_ref, gq_ref, (kv3_ref,), 3):
        mixed_ref[:, cols] = part_ref[:, cols] + acc
    gated = (layer_norm(mixed_ref[...], gain_ref[...]) * gq_ref[:, :D].astype(F32)).astype(BF16)
    out_ref[...] = tok_ref[...].astype(F32) + matmul(gated, wout_ref[...])


def attend(grp, lengths, own_tokens, gq, kvs, out_gain, w_out):
    outs = jax.ShapeDtypeStruct((TOK, D), F32)
    part = vmem_call(near_body, outs, n_smem=2, flops=10**9, moved=4 * 2**20, name="attend_near")(
        grp, lengths, gq, *kvs[:3]
    )
    return vmem_call(
        last_body, outs, n_smem=2, scratch=[pltpu.VMEM((TOK, D), F32)], flops=ATTEND_COST, moved=8 * 2**20, name="attend_last"
    )(grp, lengths, own_tokens, gq, part, kvs[3], out_gain, w_out)


def gate_of(u):
    t = jnp.tanh(u)
    return t, jnp.exp(GATE_SCALE * t)


def split(values):
    high = values.astype(BF16).astype(F32)
    return high, values - high


def split_rows(values):
    high, rest = split(values)
    middle, low = split(rest)
    return jnp.concatenate([high, middle, low], 0).astype(BF16)


def loss_body(
    query_ref, near_ref, far_ref, place_ref, back_ref, wqt_ref, wxt_ref,
    loss_ref, qgrad_ref, grads_ref,
    x_ref, unit_ref, cos_ref, dcos_ref, dcosr_ref, side_ref, dqgate_ref, dxgate_ref, dx_ref, du_ref,
):
    lanes = lax.broadcasted_iota(jnp.int32, (NEG + TOK, HALF_ROWS), 1)
    hot_near = (place_ref[...] == lanes).astype(F32).astype(BF16)
    hot_far = (place_ref[...] == lanes + HALF_ROWS).astype(F32).astype(BF16)
    x_ref[...] = (matmul(hot_near, near_ref[...]) + matmul(hot_far, far_ref[...])).astype(BF16)

    part_of = lax.broadcasted_iota(jnp.int32, (16, D), 1) // PW
    pick = (part_of == lax.broadcasted_iota(jnp.int32, (16, D), 0)).astype(F32).astype(BF16)
    eye = lax.broadcasted_iota(jnp.int32, (1, PARTS_SIZE), 1)

    rows = x_ref[...].astype(F32)
    high, low = split(rows * rows)
    squares = matmul_nt(high.astype(BF16), pick) + matmul_nt(low.astype(BF16), pick)
    x_norms = lax.rsqrt(squares[:, :PARTS_SIZE] + 1e-06)
    terms = matmul_nt(x_ref[...], split_rows(wxt_ref[...]))
    xgate = terms[:, :8] + terms[:, 8:16] + terms[:, 16:]
    side = jnp.concatenate([xgate[:NEG], x_norms[:NEG], jnp.zeros((NEG, 112), F32)], 1)
    side_ref[...] = jnp.transpose(side)[:16, :]
    pgate = xgate[NEG:]

    query = query_ref[...]
    qgate = matmul_nt(query, wqt_ref[...], HIGHEST)

    pos_cos = jnp.zeros((TOK, PARTS_SIZE), F32)
    q_norms = []
    for p in range(PARTS_SIZE):
        cols = slice(p * PW, (p + 1) * PW)
        q_p = query_ref[:, cols]
        q_norm = lax.rsqrt(jnp.sum(q_p * q_p, -1, keepdims=True) + 1e-06)
        q_unit = q_p * q_norm
        unit_ref[:, cols] = q_unit
        q_high, q_low = split(q_unit)
        x_p = x_ref[:NEG, cols]
        q_two = jnp.concatenate([q_high.astype(BF16), q_low.astype(BF16)], 1)
        cos_ref[p] = matmul_nt(q_two, jnp.concatenate([x_p, x_p], 1)) * side_ref[8 + p : 9 + p, :]
        dot_p = jnp.sum(q_unit * x_ref[NEG:, cols].astype(F32), -1, keepdims=True)
        pos_cos = jnp.where(eye == p, dot_p, pos_cos)
        q_norms.append(q_norm)
    pos_cos = pos_cos * x_norms[NEG:]

    t_pos, e_pos = gate_of(qgate + pgate)
    mix_pos = e_pos / jnp.sum(e_pos, -1, keepdims=True)
    mean_pos = jnp.sum(mix_pos * pos_cos, -1, keepdims=True)
    pos_logit = INV_TEMP * mean_pos
    raised_pos = jnp.exp(pos_logit)

    dxgate_ref[...] = jnp.zeros_like(dxgate_ref)
    dqgate_ref[...] = qgate
    loss_ref[...] = raised_pos

    def tile(i, carry):
        rows = pl.ds(pl.multiple_of(i * TILE, TILE), TILE)
        qg = dqgate_ref[rows, :]
        qgs = [jnp.broadcast_to(qg[:, p : p + 1], (TILE, PW)) for p in range(PARTS_SIZE)]
        sums = [jnp.zeros((TILE, PW), F32) for _ in range(PARTS_SIZE)]
        part = jnp.zeros((TILE, PW), F32)
        for block in range(NEG // PW):
            cols = slice(block * PW, (block + 1) * PW)
            ts, es, cs = [], [], []
            total = jnp.zeros((TILE, PW), F32)
            mixed = jnp.zeros((TILE, PW), F32)
            for p in range(PARTS_SIZE):
                t, e = gate_of(qgs[p] + side_ref[p : p + 1, cols])
                c = cos_ref[p, rows, cols]
                total = total + e
                mixed = mixed + e * c
                ts.append(t)
                es.append(e)
                cs.append(c)
            inverse = 1.0 / total
            mean = mixed * inverse
            raised = jnp.exp(INV_TEMP * mean)
            part = part + raised
            scaled = raised * inverse
            for p in range(PARTS_SIZE):
                dcos = scaled * es[p]
                du = dcos * (cs[p] - mean) * (1.0 - ts[p] * ts[p])
                dcos_ref[p, rows, cols] = dcos.astype(BF16)
                dcosr_ref[p, rows, cols] = (dcos * side_ref[8 + p : 9 + p, cols]).astype(BF16)
                du_ref[p, :, cols] = du
                sums[p] = sums[p] + du
        partition = loss_ref[rows, :] + jnp.sum(part, -1, keepdims=True)
        factor = (GATE_SCALE * INV_TEMP) / partition
        dq = jnp.zeros((TILE, PARTS_SIZE), F32)
        for p in range(PARTS_SIZE):
            du = du_ref[p] * factor
            dxgate_ref[p] += du[:8] + du[8:]
            dq = jnp.where(eye == p, jnp.sum(sums[p], -1, keepdims=True), dq)
        dqgate_ref[rows, :] = dq * factor
        loss_ref[rows, :] = partition
        return carry

    lax.fori_loop(0, TOK // TILE, tile, 0, unroll=2)

    partition = loss_ref[...]
    loss_ref[...] = jnp.log(partition) - pos_logit
    share = INV_TEMP / partition
    dpos = INV_TEMP * (raised_pos / partition - 1.0)
    dcos_pos = dpos * mix_pos
    du_pos = dcos_pos * (pos_cos - mean_pos) * (GATE_SCALE - GATE_SCALE * t_pos * t_pos)
    dxgate = jnp.transpose(jnp.concatenate([jnp.sum(dxgate_ref[...], 1), jnp.zeros((120, NEG), F32)], 0))

    def by_gate(values):
        high, low = split(values)
        return jnp.concatenate([high, low, high], 1).astype(BF16)

    def gate_weights(values):
        high, low = split(values)
        return jnp.concatenate([high, high, low], 0).astype(BF16)

    dqgate = by_gate(dqgate_ref[...] + du_pos)
    dxgate = by_gate(jnp.concatenate([dxgate[:, :PARTS_SIZE], du_pos], 0))
    wq = gate_weights(wqt_ref[...])
    wx = gate_weights(wxt_ref[...])

    for p in range(PARTS_SIZE):
        cols = slice(p * PW, (p + 1) * PW)
        q_unit = unit_ref[:, cols]
        dc = dcos_pos[:, p : p + 1]
        p_norm = x_norms[NEG:, p : p + 1]
        p_unit = x_ref[NEG:, cols].astype(F32) * p_norm
        d_unit = matmul(dcosr_ref[p], x_ref[:NEG, cols]) * share + dc * p_unit
        along = jnp.sum(d_unit * q_unit, -1, keepdims=True)
        qgrad_ref[:, cols] = (q_norms[p] * (d_unit - q_unit * along) + matmul(dqgate, wq[:, cols])).astype(BF16)

        gate_term = matmul(dxgate, wx[:, cols])
        dpos_p = p_norm * dc * (q_unit - p_unit * pos_cos[:, p : p + 1]) + gate_term[NEG:]
        dx_ref[NEG:, cols] = dpos_p.astype(BF16)

        x_norm = x_norms[:NEG, p : p + 1]
        x_unit = x_ref[:NEG, cols].astype(F32) * x_norm
        d_unit = matmul_tn(dcos_ref[p], (q_unit * share).astype(BF16))
        along = jnp.sum(d_unit * x_unit, -1, keepdims=True)
        dx_ref[:NEG, cols] = (x_norm * (d_unit - x_unit * along) + gate_term[:NEG]).astype(BF16)

    for part in range(4):
        size = 2 * HALF_ROWS // 4
        row = lax.broadcasted_iota(jnp.int32, (size, NEG + TOK), 0) + part * size
        hot = (back_ref[...] == row).astype(F32).astype(BF16)
        grads_ref[part * size : (part + 1) * size, :] = matmul(hot, dx_ref[...]).astype(BF16)


def loss_and_grads(query, near, far, place, back, w_qgate, w_xgate):
    outs = (
        jax.ShapeDtypeStruct((TOK, 1), F32),
        jax.ShapeDtypeStruct((TOK, D), BF16),
        jax.ShapeDtypeStruct((2 * HALF_ROWS, D), BF16),
    )
    scratch = [
        pltpu.VMEM((NEG + TOK, D), BF16),
        pltpu.VMEM((TOK, D), F32),
        pltpu.VMEM((PARTS_SIZE, TOK, NEG), F32),
        pltpu.VMEM((PARTS_SIZE, TOK, NEG), BF16),
        pltpu.VMEM((PARTS_SIZE, TOK, NEG), BF16),
        pltpu.VMEM((2 * PARTS_SIZE, NEG), F32),
        pltpu.VMEM((TOK, PARTS_SIZE), F32),
        pltpu.VMEM((PARTS_SIZE, 8, NEG), F32),
        pltpu.VMEM((NEG + TOK, D), BF16),
        pltpu.VMEM((PARTS_SIZE, TILE, NEG), F32),
    ]
    return vmem_call(loss_body, outs, scratch=scratch, flops=8 * 10**9, moved=10 * 2**20, name="loss")(
        query, near, far, place.reshape(-1, 1), back, w_qgate.T, w_xgate.T
    )


def local(
    tokens,
    lengths,
    in_gain,
    out_gain,
    w_in,
    w_out,
    w_qgate,
    w_xgate,
    item_table,
    neg_owner,
    neg_slot,
    pos_owner,
    pos_slot,
):
    own_tokens = tokens[0]
    half = lax.axis_index("zh").astype(jnp.int32)[None]
    grp = lax.axis_index("grp").astype(jnp.int32)[None]
    barrier = lax.optimization_barrier

    quarter = lax.dynamic_slice_in_dim(item_table, grp[0] * QUARTER, QUARTER, 0)
    tables = lax.all_gather(quarter, COLUMN, tiled=True)

    gate_query, key_value = front_kernel(own_tokens, in_gain[None], w_in)
    kvs = [key_value]
    for _ in range(2):
        kvs.append(lax.ppermute(kvs[-1], "grp", [(i, i + 1) for i in range(3)]))

    half_then, _ = barrier((half, key_value))
    ask, place, back = pack(
        half_then,
        neg_owner.reshape(1, NEG),
        neg_slot.reshape(1, NEG),
        pos_owner.reshape(1, TOK),
        pos_slot.reshape(1, TOK),
    )
    asked = lax.all_to_all(ask, PLANE, split_axis=0, concat_axis=0, tiled=True)

    asked_then, _ = barrier((asked, key_value))
    near_ids = asked_then[:, :CAP].reshape(-1, 1)
    far_ids = asked_then[:, CAP:].reshape(-1, 1)
    looked = look(near_ids, item_table)
    near = lax.all_to_all(looked, PLANE, split_axis=0, concat_axis=0, tiled=True)

    far_ids, _ = barrier((far_ids, kvs[1]))
    far_table = lax.dynamic_slice_in_dim(tables, (1 - half[0]) * ITEMS, ITEMS, 0)
    looked = look(far_ids, far_table, 20)
    far = lax.all_to_all(looked, PLANE, split_axis=0, concat_axis=0, tiled=True)

    kvs[2], _ = barrier((kvs[2], looked))
    kvs.append(lax.ppermute(kvs[2], "grp", [(i, i + 1) for i in range(3)]))
    query = attend(grp, lengths, own_tokens, gate_query, kvs, out_gain[None], w_out)

    losses, query_grad, grads = loss_and_grads(query, near, far, place, back, w_qgate, w_xgate)

    came = lax.all_to_all(grads, PLANE, split_axis=0, concat_axis=0, tiled=True)
    shard = half[0] ^ (lax.broadcasted_iota(jnp.int32, asked.shape, 1) // CAP)
    row = (asked + shard * ITEMS - (half[0] * 4 + grp[0]) * QUARTER) & (2 * ITEMS - 1)
    pieces = add_up(jnp.where(asked >= 0, row, -1).reshape(1, -1), came)
    sums = [ring_sum(pieces[8 * part : 8 * part + 8]) for part in range(len(WIDTHS))]
    return (losses.reshape(1, TOK), query_grad[None], spread(grp, sum((relay(part) for part in sums), [])))


def solution(mesh):
    fine = Mesh(mesh.devices.reshape(4, 4, 2, 4, 2), ("grp", "y", "zh", "x", "core"))
    in_specs = (
        P(SEQ, "grp", None),
        P(SEQ, None),
        P(),
        P(),
        P(),
        P(),
        P(),
        P(),
        P(SEQ, None),
        P(SEQ, "grp", None),
        P(SEQ, "grp"),
        P(SEQ, "grp", None),
        P(SEQ, "grp"),
    )
    out_specs = (P(SEQ, "grp"), P(SEQ, "grp", None), P(SEQ, None))
    return jax.shard_map(local, mesh=fine, in_specs=in_specs, out_specs=out_specs, check_vma=False)
```

```python
import math

import jax
import jax.numpy as jnp
from jax import lax
from jax.experimental import pallas as pl
from jax.experimental.pallas import tpu as pltpu
from jax.sharding import Mesh
from jax.sharding import PartitionSpec as P

HEADS = 4
PARTS_SIZE = 8
INV_TEMP = 32.0
GATE_SCALE = 2.0

D = 1024
TOK = 256
NEG = 512
ITEMS = 512
CAPN = 16
CAPP = 8
CAP = CAPN + CAPP
PEERS = 32
HALF_ROWS = PEERS * CAP
QUARTER = ITEMS // 4
WIDTHS = (512, 512)
ATTEND_COST = 8 * 10**9
QKW = 256
PW = D // PARTS_SIZE
TILE = 16

PLANE = ("y", "x", "core")
SEQ = ("y", "zh", "x", "core")
COLUMN = ("zh", "grp")

F32 = jnp.float32
BF16 = jnp.bfloat16
HIGHEST = lax.Precision.HIGHEST


def matmul(a, b):
    return jnp.dot(a, b, preferred_element_type=F32)


def matmul_nt(a, b, precision=None):
    return lax.dot_general(a, b, (((1,), (1,)), ((), ())), precision=precision, preferred_element_type=F32)


def matmul_tn(a, b, precision=None):
    return lax.dot_general(a, b, (((0,), (0,)), ((), ())), precision=precision, preferred_element_type=F32)


def vmem_call(body, outs, n_smem=0, n_any=0, scratch=(), limit=50, flops=0, moved=0, name=None):
    def call(*args):
        in_specs = [pl.BlockSpec(memory_space=pltpu.SMEM)] * n_smem
        in_specs += [pl.BlockSpec(memory_space=pl.ANY)] * n_any
        in_specs += [pl.BlockSpec(memory_space=pltpu.VMEM)] * (len(args) - n_smem - n_any)
        return pl.pallas_call(
            body,
            out_shape=outs,
            in_specs=in_specs,
            out_specs=jax.tree.map(lambda _: pl.BlockSpec(memory_space=pltpu.VMEM), outs),
            scratch_shapes=list(scratch),
            compiler_params=pltpu.CompilerParams(vmem_limit_bytes=limit * 2**20),
            cost_estimate=pl.CostEstimate(flops=flops, bytes_accessed=moved, transcendentals=0),
            name=name,
        )(*args)

    return call


def pack_body(half_ref, nown_ref, nslot_ref, pown_ref, pslot_ref, ask_ref, place_ref, back_ref, owner_ref, slot_ref, sems):
    total = NEG + TOK
    pairs = (
        (nown_ref, owner_ref.at[:, :NEG]),
        (nslot_ref, slot_ref.at[:, :NEG]),
        (pown_ref, owner_ref.at[:, NEG:]),
        (pslot_ref, slot_ref.at[:, NEG:]),
    )
    copies = [pltpu.make_async_copy(a, b, sems.at[i]) for i, (a, b) in enumerate(pairs)]
    for copy in copies:
        copy.start()
    for copy in copies:
        copy.wait()
    owner = owner_ref[...]
    slot = slot_ref[...]
    lane = lax.broadcasted_iota(jnp.int32, (1, total), 1)
    positive = (lane >= NEG).astype(jnp.int32)
    far = ((owner >> 3) & 1) ^ half_ref[0]
    peer = (owner >> 4) * 8 + (owner & 7)
    key = positive * 64 + far * 32 + peer
    hot = key == lax.broadcasted_iota(jnp.int32, (128, total), 0)
    before = lax.broadcasted_iota(jnp.int32, (total, total), 0) < lax.broadcasted_iota(jnp.int32, (total, total), 1)
    counts = matmul(hot.astype(F32).astype(BF16), before.astype(F32).astype(BF16))
    rank = jnp.sum(jnp.where(hot, counts, 0.0), 0, keepdims=True).astype(jnp.int32)
    inner = rank + positive * CAPN
    column = far * CAP + inner
    peer_hot = (peer == lax.broadcasted_iota(jnp.int32, (PEERS, total), 0)).astype(F32).astype(BF16)
    here = column == lax.broadcasted_iota(jnp.int32, (2 * CAP, total), 0)
    value = slot + 1
    high = jnp.where(here, (value >> 5).astype(F32), 0.0).astype(BF16)
    low = jnp.where(here, (value & 31).astype(F32), 0.0).astype(BF16)
    ids = matmul_nt(peer_hot, high) * 32.0 + matmul_nt(peer_hot, low)
    ask_ref[...] = ids.astype(jnp.int32) - 1
    place_ref[...] = far * HALF_ROWS + peer * CAP + inner
    back_ref[...] = peer * (2 * CAP) + column


def pack(half, neg_owner, neg_slot, pos_owner, pos_slot):
    outs = (
        jax.ShapeDtypeStruct((PEERS, 2 * CAP), jnp.int32),
        jax.ShapeDtypeStruct((1, NEG + TOK), jnp.int32),
        jax.ShapeDtypeStruct((1, NEG + TOK), jnp.int32),
    )
    row = pltpu.VMEM((1, NEG + TOK), jnp.int32)
    return vmem_call(
        pack_body, outs, n_smem=1, n_any=4, scratch=[row, row, pltpu.SemaphoreType.DMA((4,))], name="pack"
    )(half, neg_owner, neg_slot, pos_owner, pos_slot)


def look_body(ids_ref, table_ref, rows_ref):
    hot = ids_ref[...] == lax.broadcasted_iota(jnp.int32, (HALF_ROWS, ITEMS), 1)
    rows_ref[...] = matmul(hot.astype(F32).astype(BF16), table_ref[...]).astype(BF16)


def look(ids, table, cost=1):
    outs = jax.ShapeDtypeStruct((HALF_ROWS, D), BF16)
    return vmem_call(look_body, outs, flops=cost * 2 * HALF_ROWS * ITEMS * D, moved=4 * 2**20, name="look")(ids, table)


def relay(own):
    up = lax.ppermute(own, "grp", [(0, 1), (1, 2), (2, 3)])
    down = lax.ppermute(own, "grp", [(1, 0), (2, 1), (3, 2)])
    two = lax.ppermute(own, "grp", [(i, (i + 2) % 4) for i in range(4)])
    end = lax.ppermute(two, "grp", [(2, 3), (1, 0)])
    return [own, up, down, two, end]


def lay_out(grp, refs, out_ref, cols):
    def put(at, ref):
        out_ref[pl.ds(pl.multiple_of(at * QUARTER, QUARTER), QUARTER), cols] = ref[...].astype(out_ref.dtype)

    own, up, down, two, end = refs
    put(grp, own)
    put((grp + 2) & 3, two)
    pl.when(grp > 0)(lambda: put(grp - 1, up))
    pl.when(grp < 3)(lambda: put(grp + 1, down))
    pl.when((grp == 0) | (grp == 3))(lambda: put(3 - grp, end))


def spread_body(grp_ref, *refs):
    out_ref = refs[-1]
    at = 0
    for i, width in enumerate(WIDTHS):
        lay_out(grp_ref[0], refs[5 * i : 5 * i + 5], out_ref, slice(at, at + width))
        at += width


def spread(grp, quarters):
    outs = jax.ShapeDtypeStruct((ITEMS, D), F32)
    return vmem_call(spread_body, outs, n_smem=1, moved=3 * 2**20, name="spread")(grp, *quarters)


def column_hop(value, step, senders):
    place = [(i % 4) * 2 + i // 4 for i in range(8)]
    pairs = [(place[i], place[(i + step) % 8]) for i in range(8) if i % 4 in senders]
    return lax.ppermute(value, ("grp", "zh"), pairs)


def add_body(ids_ref, grads_ref, *piece_refs):
    eighth = 2 * ITEMS // 8
    for pair in range(4):
        row = lax.broadcasted_iota(jnp.int32, (2 * eighth, 2 * HALF_ROWS), 0) + pair * 2 * eighth
        hot = (ids_ref[...] == row).astype(F32).astype(BF16)
        summed = matmul(hot, grads_ref[...]).astype(BF16)
        for i in range(2):
            at = 0
            for part, width in enumerate(WIDTHS):
                ref = piece_refs[8 * part + 2 * pair + i]
                ref[...] = summed[i * eighth : (i + 1) * eighth, at : at + width]
                at += width


def add_up(ids, grads):
    outs = sum(((jax.ShapeDtypeStruct((ITEMS // 4, width), BF16),) * 8 for width in WIDTHS), ())
    return vmem_call(add_body, outs, flops=8 * HALF_ROWS * ITEMS * D, moved=5 * 2**20, name="add_up")(ids, grads)


def ring_sum(pieces):
    def hop(value, step):
        return column_hop(value, step, range(4))

    def plus(value, piece):
        return (value.astype(F32) + piece.astype(F32)).astype(BF16)

    back = hop(pieces[4], -1)
    ahead = hop(pieces[3], 1)
    back = hop(plus(back, pieces[5]), -1)
    ahead = hop(plus(ahead, pieces[2]), 1)
    back = hop(plus(back, pieces[6]), -1)
    ahead = hop(plus(ahead, pieces[1]), 1)
    back = hop(plus(back, pieces[7]), -1)
    return (pieces[0].astype(F32) + back.astype(F32) + ahead.astype(F32)).astype(BF16)


def layer_norm(values, gain_vec):
    average = jnp.mean(values, -1, keepdims=True)
    centred = values - average
    spread = jnp.mean(centred * centred, -1, keepdims=True)
    return centred * lax.rsqrt(spread + 1e-05) * gain_vec


def front_body(tok_ref, gain_ref, w_ref, gq_ref, kv_ref):
    normed = layer_norm(tok_ref[...].astype(F32), gain_ref[...]).astype(BF16)

    def project(first, size):
        half = 0.5 * matmul(normed, w_ref[:, first : first + size])
        return (half + half * jnp.tanh(half)).astype(BF16)

    for at in range(0, D, 512):
        kv_ref[:, at : at + 512] = project(D + at, 512)
    kv_ref[:, D:] = project(2 * D + QKW, QKW)
    for at in range(0, D, 512):
        gq_ref[:, at : at + 512] = project(at, 512)
    gq_ref[:, D:] = project(2 * D, QKW)


def front_kernel(own_tokens, in_gain, w_in):
    out = jax.ShapeDtypeStruct((TOK, D + QKW), BF16)
    return vmem_call(front_body, (out, out), flops=14 * 10**8, moved=7 * 2**20, name="front")(own_tokens, in_gain, w_in)


def attend_blocks(grp_ref, len_ref, gq_ref, kv_refs, first):
    start = grp_ref[0] * TOK
    ends = [len_ref[0, 0]]
    for i in range(1, len_ref.shape[1]):
        ends.append(ends[-1] + len_ref[0, i])

    def segment(pos):
        return sum((pos >= end).astype(jnp.int32) for end in ends)

    query_pos = start + lax.broadcasted_iota(jnp.int32, (TOK, 1), 0)
    query_seg = segment(query_pos)
    masks = []
    for hop in range(first, first + len(kv_refs)):
        key_pos = start - hop * TOK + lax.broadcasted_iota(jnp.int32, (1, TOK), 1)
        seen = (query_seg == segment(key_pos)) & (key_pos >= 0) & (key_pos <= query_pos)
        masks.append(jnp.where(seen, 0.5 / math.sqrt(QKW // HEADS), 0.0))
    qkh = QKW // HEADS
    vh = D // HEADS
    for head in range(HEADS):
        query = gq_ref[:, D + head * qkh : D + (head + 1) * qkh]
        acc = jnp.zeros((TOK, vh), F32)
        for mask, ref in zip(masks, kv_refs):
            key = ref[:, D + head * qkh : D + (head + 1) * qkh]
            value = ref[:, head * vh : (head + 1) * vh]
            scores = matmul_nt(query, key) * mask
            weights = (scores + scores * jnp.tanh(scores)).astype(BF16)
            acc = acc + matmul(weights, value)
        yield slice(head * vh, (head + 1) * vh), acc


def near_body(grp_ref, len_ref, gq_ref, kv0_ref, kv1_ref, kv2_ref, mixed_ref):
    for cols, acc in attend_blocks(grp_ref, len_ref, gq_ref, (kv0_ref, kv1_ref, kv2_ref), 0):
        mixed_ref[:, cols] = acc


def last_body(grp_ref, len_ref, tok_ref, gq_ref, part_ref, kv3_ref, gain_ref, wout_ref, out_ref, mixed_ref):
    for cols, acc in attend_blocks(grp_ref, len_ref, gq_ref, (kv3_ref,), 3):
        mixed_ref[:, cols] = part_ref[:, cols] + acc
    gated = (layer_norm(mixed_ref[...], gain_ref[...]) * gq_ref[:, :D].astype(F32)).astype(BF16)
    out_ref[...] = tok_ref[...].astype(F32) + matmul(gated, wout_ref[...])


def attend(grp, lengths, own_tokens, gq, kvs, out_gain, w_out):
    outs = jax.ShapeDtypeStruct((TOK, D), F32)
    part = vmem_call(near_body, outs, n_smem=2, flops=10**9, moved=4 * 2**20, name="attend_near")(
        grp, lengths, gq, *kvs[:3]
    )
    return vmem_call(
        last_body, outs, n_smem=2, scratch=[pltpu.VMEM((TOK, D), F32)], flops=ATTEND_COST, moved=8 * 2**20, name="attend_last"
    )(grp, lengths, own_tokens, gq, part, kvs[3], out_gain, w_out)


def gate_of(u):
    t = jnp.tanh(u)
    return t, jnp.exp(GATE_SCALE * t)


def split(values):
    high = values.astype(BF16).astype(F32)
    return high, values - high


def split_rows(values):
    high, rest = split(values)
    middle, low = split(rest)
    return jnp.concatenate([high, middle, low], 0).astype(BF16)


def loss_body(
    query_ref, near_ref, far_ref, place_ref, back_ref, wqt_ref, wxt_ref,
    loss_ref, qgrad_ref, grads_ref,
    x_ref, unit_ref, cos_ref, dcos_ref, dcosr_ref, side_ref, dqgate_ref, dxgate_ref, dx_ref, du_ref,
):
    lanes = lax.broadcasted_iota(jnp.int32, (NEG + TOK, HALF_ROWS), 1)
    hot_near = (place_ref[...] == lanes).astype(F32).astype(BF16)
    hot_far = (place_ref[...] == lanes + HALF_ROWS).astype(F32).astype(BF16)
    x_ref[...] = (matmul(hot_near, near_ref[...]) + matmul(hot_far, far_ref[...])).astype(BF16)

    part_of = lax.broadcasted_iota(jnp.int32, (16, D), 1) // PW
    pick = (part_of == lax.broadcasted_iota(jnp.int32, (16, D), 0)).astype(F32).astype(BF16)
    eye = lax.broadcasted_iota(jnp.int32, (1, PARTS_SIZE), 1)

    rows = x_ref[...].astype(F32)
    high, low = split(rows * rows)
    squares = matmul_nt(high.astype(BF16), pick) + matmul_nt(low.astype(BF16), pick)
    x_norms = lax.rsqrt(squares[:, :PARTS_SIZE] + 1e-06)
    terms = matmul_nt(x_ref[...], split_rows(wxt_ref[...]))
    xgate = terms[:, :8] + terms[:, 8:16] + terms[:, 16:]
    side = jnp.concatenate([xgate[:NEG], x_norms[:NEG], jnp.zeros((NEG, 112), F32)], 1)
    side_ref[...] = jnp.transpose(side)[:16, :]
    pgate = xgate[NEG:]

    query = query_ref[...]
    qgate = matmul_nt(query, wqt_ref[...], HIGHEST)

    pos_cos = jnp.zeros((TOK, PARTS_SIZE), F32)
    q_norms = []
    for p in range(PARTS_SIZE):
        cols = slice(p * PW, (p + 1) * PW)
        q_p = query_ref[:, cols]
        q_norm = lax.rsqrt(jnp.sum(q_p * q_p, -1, keepdims=True) + 1e-06)
        q_unit = q_p * q_norm
        unit_ref[:, cols] = q_unit
        q_high, q_low = split(q_unit)
        x_p = x_ref[:NEG, cols]
        q_two = jnp.concatenate([q_high.astype(BF16), q_low.astype(BF16)], 1)
        cos_ref[p] = matmul_nt(q_two, jnp.concatenate([x_p, x_p], 1)) * side_ref[8 + p : 9 + p, :]
        dot_p = jnp.sum(q_unit * x_ref[NEG:, cols].astype(F32), -1, keepdims=True)
        pos_cos = jnp.where(eye == p, dot_p, pos_cos)
        q_norms.append(q_norm)
    pos_cos = pos_cos * x_norms[NEG:]

    t_pos, e_pos = gate_of(qgate + pgate)
    mix_pos = e_pos / jnp.sum(e_pos, -1, keepdims=True)
    mean_pos = jnp.sum(mix_pos * pos_cos, -1, keepdims=True)
    pos_logit = INV_TEMP * mean_pos
    raised_pos = jnp.exp(pos_logit)

    dxgate_ref[...] = jnp.zeros_like(dxgate_ref)
    dqgate_ref[...] = qgate
    loss_ref[...] = raised_pos

    def tile(i, carry):
        rows = pl.ds(pl.multiple_of(i * TILE, TILE), TILE)
        qg = dqgate_ref[rows, :]
        qgs = [jnp.broadcast_to(qg[:, p : p + 1], (TILE, PW)) for p in range(PARTS_SIZE)]
        sums = [jnp.zeros((TILE, PW), F32) for _ in range(PARTS_SIZE)]
        part = jnp.zeros((TILE, PW), F32)
        for block in range(NEG // PW):
            cols = slice(block * PW, (block + 1) * PW)
            ts, es, cs = [], [], []
            total = jnp.zeros((TILE, PW), F32)
            mixed = jnp.zeros((TILE, PW), F32)
            for p in range(PARTS_SIZE):
                t, e = gate_of(qgs[p] + side_ref[p : p + 1, cols])
                c = cos_ref[p, rows, cols]
                total = total + e
                mixed = mixed + e * c
                ts.append(t)
                es.append(e)
                cs.append(c)
            inverse = 1.0 / total
            mean = mixed * inverse
            raised = jnp.exp(INV_TEMP * mean)
            part = part + raised
            scaled = raised * inverse
            for p in range(PARTS_SIZE):
                dcos = scaled * es[p]
                du = dcos * (cs[p] - mean) * (1.0 - ts[p] * ts[p])
                dcos_ref[p, rows, cols] = dcos.astype(BF16)
                dcosr_ref[p, rows, cols] = (dcos * side_ref[8 + p : 9 + p, cols]).astype(BF16)
                du_ref[p, :, cols] = du
                sums[p] = sums[p] + du
        partition = loss_ref[rows, :] + jnp.sum(part, -1, keepdims=True)
        factor = (GATE_SCALE * INV_TEMP) / partition
        dq = jnp.zeros((TILE, PARTS_SIZE), F32)
        for p in range(PARTS_SIZE):
            du = du_ref[p] * factor
            dxgate_ref[p] += du[:8] + du[8:]
            dq = jnp.where(eye == p, jnp.sum(sums[p], -1, keepdims=True), dq)
        dqgate_ref[rows, :] = dq * factor
        loss_ref[rows, :] = partition
        return carry

    lax.fori_loop(0, TOK // TILE, tile, 0, unroll=2)

    partition = loss_ref[...]
    loss_ref[...] = jnp.log(partition) - pos_logit
    share = INV_TEMP / partition
    dpos = INV_TEMP * (raised_pos / partition - 1.0)
    dcos_pos = dpos * mix_pos
    du_pos = dcos_pos * (pos_cos - mean_pos) * (GATE_SCALE - GATE_SCALE * t_pos * t_pos)
    dxgate = jnp.transpose(jnp.concatenate([jnp.sum(dxgate_ref[...], 1), jnp.zeros((120, NEG), F32)], 0))

    def by_gate(values):
        high, low = split(values)
        return jnp.concatenate([high, low, high], 1).astype(BF16)

    def gate_weights(values):
        high, low = split(values)
        return jnp.concatenate([high, high, low], 0).astype(BF16)

    dqgate = by_gate(dqgate_ref[...] + du_pos)
    dxgate = by_gate(jnp.concatenate([dxgate[:, :PARTS_SIZE], du_pos], 0))
    wq = gate_weights(wqt_ref[...])
    wx = gate_weights(wxt_ref[...])

    for p in range(PARTS_SIZE):
        cols = slice(p * PW, (p + 1) * PW)
        q_unit = unit_ref[:, cols]
        dc = dcos_pos[:, p : p + 1]
        p_norm = x_norms[NEG:, p : p + 1]
        p_unit = x_ref[NEG:, cols].astype(F32) * p_norm
        d_unit = matmul(dcosr_ref[p], x_ref[:NEG, cols]) * share + dc * p_unit
        along = jnp.sum(d_unit * q_unit, -1, keepdims=True)
        qgrad_ref[:, cols] = (q_norms[p] * (d_unit - q_unit * along) + matmul(dqgate, wq[:, cols])).astype(BF16)

        gate_term = matmul(dxgate, wx[:, cols])
        dpos_p = p_norm * dc * (q_unit - p_unit * pos_cos[:, p : p + 1]) + gate_term[NEG:]
        dx_ref[NEG:, cols] = dpos_p.astype(BF16)

        x_norm = x_norms[:NEG, p : p + 1]
        x_unit = x_ref[:NEG, cols].astype(F32) * x_norm
        d_unit = matmul_tn(dcos_ref[p], (q_unit * share).astype(BF16))
        along = jnp.sum(d_unit * x_unit, -1, keepdims=True)
        dx_ref[:NEG, cols] = (x_norm * (d_unit - x_unit * along) + gate_term[:NEG]).astype(BF16)

    for part in range(4):
        size = 2 * HALF_ROWS // 4
        row = lax.broadcasted_iota(jnp.int32, (size, NEG + TOK), 0) + part * size
        hot = (back_ref[...] == row).astype(F32).astype(BF16)
        grads_ref[part * size : (part + 1) * size, :] = matmul(hot, dx_ref[...]).astype(BF16)


def loss_and_grads(query, near, far, place, back, w_qgate, w_xgate):
    outs = (
        jax.ShapeDtypeStruct((TOK, 1), F32),
        jax.ShapeDtypeStruct((TOK, D), BF16),
        jax.ShapeDtypeStruct((2 * HALF_ROWS, D), BF16),
    )
    scratch = [
        pltpu.VMEM((NEG + TOK, D), BF16),
        pltpu.VMEM((TOK, D), F32),
        pltpu.VMEM((PARTS_SIZE, TOK, NEG), F32),
        pltpu.VMEM((PARTS_SIZE, TOK, NEG), BF16),
        pltpu.VMEM((PARTS_SIZE, TOK, NEG), BF16),
        pltpu.VMEM((2 * PARTS_SIZE, NEG), F32),
        pltpu.VMEM((TOK, PARTS_SIZE), F32),
        pltpu.VMEM((PARTS_SIZE, 8, NEG), F32),
        pltpu.VMEM((NEG + TOK, D), BF16),
        pltpu.VMEM((PARTS_SIZE, TILE, NEG), F32),
    ]
    return vmem_call(loss_body, outs, scratch=scratch, flops=8 * 10**9, moved=10 * 2**20, name="loss")(
        query, near, far, place.reshape(-1, 1), back, w_qgate.T, w_xgate.T
    )


def local(
    tokens,
    lengths,
    in_gain,
    out_gain,
    w_in,
    w_out,
    w_qgate,
    w_xgate,
    item_table,
    neg_owner,
    neg_slot,
    pos_owner,
    pos_slot,
):
    own_tokens = tokens[0]
    half = lax.axis_index("zh").astype(jnp.int32)[None]
    grp = lax.axis_index("grp").astype(jnp.int32)[None]
    barrier = lax.optimization_barrier

    quarter = lax.dynamic_slice_in_dim(item_table, grp[0] * QUARTER, QUARTER, 0)
    tables = lax.all_gather(quarter, COLUMN, tiled=True)

    gate_query, key_value = front_kernel(own_tokens, in_gain[None], w_in)
    kvs = [key_value]
    for _ in range(2):
        kvs.append(lax.ppermute(kvs[-1], "grp", [(i, i + 1) for i in range(3)]))

    half_then, _ = barrier((half, key_value))
    ask, place, back = pack(
        half_then,
        neg_owner.reshape(1, NEG),
        neg_slot.reshape(1, NEG),
        pos_owner.reshape(1, TOK),
        pos_slot.reshape(1, TOK),
    )
    asked = lax.all_to_all(ask, PLANE, split_axis=0, concat_axis=0, tiled=True)

    asked_then, _ = barrier((asked, key_value))
    near_ids = asked_then[:, :CAP].reshape(-1, 1)
    far_ids = asked_then[:, CAP:].reshape(-1, 1)
    looked = look(near_ids, item_table)
    near = lax.all_to_all(looked, PLANE, split_axis=0, concat_axis=0, tiled=True)

    far_ids, _ = barrier((far_ids, kvs[1]))
    far_table = lax.dynamic_slice_in_dim(tables, (1 - half[0]) * ITEMS, ITEMS, 0)
    looked = look(far_ids, far_table, 20)
    far = lax.all_to_all(looked, PLANE, split_axis=0, concat_axis=0, tiled=True)

    kvs[2], _ = barrier((kvs[2], looked))
    kvs.append(lax.ppermute(kvs[2], "grp", [(i, i + 1) for i in range(3)]))
    query = attend(grp, lengths, own_tokens, gate_query, kvs, out_gain[None], w_out)

    losses, query_grad, grads = loss_and_grads(query, near, far, place, back, w_qgate, w_xgate)

    came = lax.all_to_all(grads, PLANE, split_axis=0, concat_axis=0, tiled=True)
    shard = half[0] ^ (lax.broadcasted_iota(jnp.int32, asked.shape, 1) // CAP)
    row = (asked + shard * ITEMS - (half[0] * 4 + grp[0]) * QUARTER) & (2 * ITEMS - 1)
    pieces = add_up(jnp.where(asked >= 0, row, -1).reshape(1, -1), came)
    sums = [ring_sum(pieces[8 * part : 8 * part + 8]) for part in range(len(WIDTHS))]
    return (losses.reshape(1, TOK), query_grad[None], spread(grp, sum((relay(part) for part in sums), [])))


def solution(mesh):
    fine = Mesh(mesh.devices.reshape(4, 4, 2, 4, 2), ("grp", "y", "zh", "x", "core"))
    in_specs = (
        P(SEQ, "grp", None),
        P(SEQ, None),
        P(),
        P(),
        P(),
        P(),
        P(),
        P(),
        P(SEQ, None),
        P(SEQ, "grp", None),
        P(SEQ, "grp"),
        P(SEQ, "grp", None),
        P(SEQ, "grp"),
    )
    out_specs = (P(SEQ, "grp"), P(SEQ, "grp", None), P(SEQ, None))
    return jax.shard_map(local, mesh=fine, in_specs=in_specs, out_specs=out_specs, check_vma=False)
```

```python
import math

import jax
import jax.numpy as jnp
from jax import lax
from jax.experimental import pallas as pl
from jax.experimental.pallas import tpu as pltpu
from jax.sharding import Mesh
from jax.sharding import PartitionSpec as P

HEADS = 4
PARTS_SIZE = 8
INV_TEMP = 32.0
GATE_SCALE = 2.0

D = 1024
TOK = 256
NEG = 512
ITEMS = 512
CAPN = 16
CAPP = 8
CAP = CAPN + CAPP
PEERS = 32
HALF_ROWS = PEERS * CAP
QUARTER = ITEMS // 4
WIDTHS = (512, 512)
ATTEND_COST = 4 * 10**10
QKW = 256
PW = D // PARTS_SIZE
TILE = 16

PLANE = ("y", "x", "core")
SEQ = ("y", "zh", "x", "core")
COLUMN = ("zh", "grp")

F32 = jnp.float32
BF16 = jnp.bfloat16
HIGHEST = lax.Precision.HIGHEST


def matmul(a, b):
    return jnp.dot(a, b, preferred_element_type=F32)


def matmul_nt(a, b, precision=None):
    return lax.dot_general(a, b, (((1,), (1,)), ((), ())), precision=precision, preferred_element_type=F32)


def matmul_tn(a, b, precision=None):
    return lax.dot_general(a, b, (((0,), (0,)), ((), ())), precision=precision, preferred_element_type=F32)


def vmem_call(body, outs, n_smem=0, n_any=0, scratch=(), limit=50, flops=0, moved=0, name=None):
    def call(*args):
        in_specs = [pl.BlockSpec(memory_space=pltpu.SMEM)] * n_smem
        in_specs += [pl.BlockSpec(memory_space=pl.ANY)] * n_any
        in_specs += [pl.BlockSpec(memory_space=pltpu.VMEM)] * (len(args) - n_smem - n_any)
        return pl.pallas_call(
            body,
            out_shape=outs,
            in_specs=in_specs,
            out_specs=jax.tree.map(lambda _: pl.BlockSpec(memory_space=pltpu.VMEM), outs),
            scratch_shapes=list(scratch),
            compiler_params=pltpu.CompilerParams(vmem_limit_bytes=limit * 2**20),
            cost_estimate=pl.CostEstimate(flops=flops, bytes_accessed=moved, transcendentals=0),
            name=name,
        )(*args)

    return call


def pack_body(half_ref, nown_ref, nslot_ref, pown_ref, pslot_ref, ask_ref, place_ref, back_ref, owner_ref, slot_ref, sems):
    total = NEG + TOK
    pairs = (
        (nown_ref, owner_ref.at[:, :NEG]),
        (nslot_ref, slot_ref.at[:, :NEG]),
        (pown_ref, owner_ref.at[:, NEG:]),
        (pslot_ref, slot_ref.at[:, NEG:]),
    )
    copies = [pltpu.make_async_copy(a, b, sems.at[i]) for i, (a, b) in enumerate(pairs)]
    for copy in copies:
        copy.start()
    for copy in copies:
        copy.wait()
    owner = owner_ref[...]
    slot = slot_ref[...]
    lane = lax.broadcasted_iota(jnp.int32, (1, total), 1)
    positive = (lane >= NEG).astype(jnp.int32)
    far = ((owner >> 3) & 1) ^ half_ref[0]
    peer = (owner >> 4) * 8 + (owner & 7)
    key = positive * 64 + far * 32 + peer
    hot = key == lax.broadcasted_iota(jnp.int32, (128, total), 0)
    before = lax.broadcasted_iota(jnp.int32, (total, total), 0) < lax.broadcasted_iota(jnp.int32, (total, total), 1)
    counts = matmul(hot.astype(F32).astype(BF16), before.astype(F32).astype(BF16))
    rank = jnp.sum(jnp.where(hot, counts, 0.0), 0, keepdims=True).astype(jnp.int32)
    inner = rank + positive * CAPN
    column = far * CAP + inner
    peer_hot = (peer == lax.broadcasted_iota(jnp.int32, (PEERS, total), 0)).astype(F32).astype(BF16)
    here = column == lax.broadcasted_iota(jnp.int32, (2 * CAP, total), 0)
    value = slot + 1
    high = jnp.where(here, (value >> 5).astype(F32), 0.0).astype(BF16)
    low = jnp.where(here, (value & 31).astype(F32), 0.0).astype(BF16)
    ids = matmul_nt(peer_hot, high) * 32.0 + matmul_nt(peer_hot, low)
    ask_ref[...] = ids.astype(jnp.int32) - 1
    place_ref[...] = far * HALF_ROWS + peer * CAP + inner
    back_ref[...] = peer * (2 * CAP) + column


def pack(half, neg_owner, neg_slot, pos_owner, pos_slot):
    outs = (
        jax.ShapeDtypeStruct((PEERS, 2 * CAP), jnp.int32),
        jax.ShapeDtypeStruct((1, NEG + TOK), jnp.int32),
        jax.ShapeDtypeStruct((1, NEG + TOK), jnp.int32),
    )
    row = pltpu.VMEM((1, NEG + TOK), jnp.int32)
    return vmem_call(
        pack_body, outs, n_smem=1, n_any=4, scratch=[row, row, pltpu.SemaphoreType.DMA((4,))], name="pack"
    )(half, neg_owner, neg_slot, pos_owner, pos_slot)


def look_body(ids_ref, table_ref, rows_ref):
    hot = ids_ref[...] == lax.broadcasted_iota(jnp.int32, (HALF_ROWS, ITEMS), 1)
    rows_ref[...] = matmul(hot.astype(F32).astype(BF16), table_ref[...]).astype(BF16)


def look(ids, table, cost=1):
    outs = jax.ShapeDtypeStruct((HALF_ROWS, D), BF16)
    return vmem_call(look_body, outs, flops=cost * 2 * HALF_ROWS * ITEMS * D, moved=4 * 2**20, name="look")(ids, table)


def relay(own):
    up = lax.ppermute(own, "grp", [(0, 1), (1, 2), (2, 3)])
    down = lax.ppermute(own, "grp", [(1, 0), (2, 1), (3, 2)])
    two = lax.ppermute(own, "grp", [(i, (i + 2) % 4) for i in range(4)])
    end = lax.ppermute(two, "grp", [(2, 3), (1, 0)])
    return [own, up, down, two, end]


def lay_out(grp, refs, out_ref, cols):
    def put(at, ref):
        out_ref[pl.ds(pl.multiple_of(at * QUARTER, QUARTER), QUARTER), cols] = ref[...].astype(out_ref.dtype)

    own, up, down, two, end = refs
    put(grp, own)
    put((grp + 2) & 3, two)
    pl.when(grp > 0)(lambda: put(grp - 1, up))
    pl.when(grp < 3)(lambda: put(grp + 1, down))
    pl.when((grp == 0) | (grp == 3))(lambda: put(3 - grp, end))


def spread_body(grp_ref, *refs):
    out_ref = refs[-1]
    at = 0
    for i, width in enumerate(WIDTHS):
        lay_out(grp_ref[0], refs[5 * i : 5 * i + 5], out_ref, slice(at, at + width))
        at += width


def spread(grp, quarters):
    outs = jax.ShapeDtypeStruct((ITEMS, D), F32)
    return vmem_call(spread_body, outs, n_smem=1, moved=3 * 2**20, name="spread")(grp, *quarters)


def column_hop(value, step, senders):
    place = [(i % 4) * 2 + i // 4 for i in range(8)]
    pairs = [(place[i], place[(i + step) % 8]) for i in range(8) if i % 4 in senders]
    return lax.ppermute(value, ("grp", "zh"), pairs)


def add_body(ids_ref, grads_ref, *piece_refs):
    eighth = 2 * ITEMS // 8
    for pair in range(4):
        row = lax.broadcasted_iota(jnp.int32, (2 * eighth, 2 * HALF_ROWS), 0) + pair * 2 * eighth
        hot = (ids_ref[...] == row).astype(F32).astype(BF16)
        summed = matmul(hot, grads_ref[...]).astype(BF16)
        for i in range(2):
            at = 0
            for part, width in enumerate(WIDTHS):
                ref = piece_refs[8 * part + 2 * pair + i]
                ref[...] = summed[i * eighth : (i + 1) * eighth, at : at + width]
                at += width


def add_up(ids, grads):
    outs = sum(((jax.ShapeDtypeStruct((ITEMS // 4, width), BF16),) * 8 for width in WIDTHS), ())
    return vmem_call(add_body, outs, flops=8 * HALF_ROWS * ITEMS * D, moved=5 * 2**20, name="add_up")(ids, grads)


def ring_sum(pieces):
    def hop(value, step):
        return column_hop(value, step, range(4))

    def plus(value, piece):
        return (value.astype(F32) + piece.astype(F32)).astype(BF16)

    back = hop(pieces[4], -1)
    ahead = hop(pieces[3], 1)
    back = hop(plus(back, pieces[5]), -1)
    ahead = hop(plus(ahead, pieces[2]), 1)
    back = hop(plus(back, pieces[6]), -1)
    ahead = hop(plus(ahead, pieces[1]), 1)
    back = hop(plus(back, pieces[7]), -1)
    return (pieces[0].astype(F32) + back.astype(F32) + ahead.astype(F32)).astype(BF16)


def layer_norm(values, gain_vec):
    average = jnp.mean(values, -1, keepdims=True)
    centred = values - average
    spread = jnp.mean(centred * centred, -1, keepdims=True)
    return centred * lax.rsqrt(spread + 1e-05) * gain_vec


def front_body(tok_ref, gain_ref, w_ref, gq_ref, kv_ref):
    normed = layer_norm(tok_ref[...].astype(F32), gain_ref[...]).astype(BF16)

    def project(first, size):
        half = 0.5 * matmul(normed, w_ref[:, first : first + size])
        return (half + half * jnp.tanh(half)).astype(BF16)

    for at in range(0, D, 512):
        kv_ref[:, at : at + 512] = project(D + at, 512)
    kv_ref[:, D:] = project(2 * D + QKW, QKW)
    for at in range(0, D, 512):
        gq_ref[:, at : at + 512] = project(at, 512)
    gq_ref[:, D:] = project(2 * D, QKW)


def front_kernel(own_tokens, in_gain, w_in):
    out = jax.ShapeDtypeStruct((TOK, D + QKW), BF16)
    return vmem_call(front_body, (out, out), flops=14 * 10**8, moved=7 * 2**20, name="front")(own_tokens, in_gain, w_in)


def attend_blocks(grp_ref, len_ref, gq_ref, kv_refs, first):
    start = grp_ref[0] * TOK
    ends = [len_ref[0, 0]]
    for i in range(1, len_ref.shape[1]):
        ends.append(ends[-1] + len_ref[0, i])

    def segment(pos):
        return sum((pos >= end).astype(jnp.int32) for end in ends)

    query_pos = start + lax.broadcasted_iota(jnp.int32, (TOK, 1), 0)
    query_seg = segment(query_pos)
    masks = []
    for hop in range(first, first + len(kv_refs)):
        key_pos = start - hop * TOK + lax.broadcasted_iota(jnp.int32, (1, TOK), 1)
        seen = (query_seg == segment(key_pos)) & (key_pos >= 0) & (key_pos <= query_pos)
        masks.append(jnp.where(seen, 0.5 / math.sqrt(QKW // HEADS), 0.0))
    qkh = QKW // HEADS
    vh = D // HEADS
    for head in range(HEADS):
        query = gq_ref[:, D + head * qkh : D + (head + 1) * qkh]
        acc = jnp.zeros((TOK, vh), F32)
        for mask, ref in zip(masks, kv_refs):
            key = ref[:, D + head * qkh : D + (head + 1) * qkh]
            value = ref[:, head * vh : (head + 1) * vh]
            scores = matmul_nt(query, key) * mask
            weights = (scores + scores * jnp.tanh(scores)).astype(BF16)
            acc = acc + matmul(weights, value)
        yield slice(head * vh, (head + 1) * vh), acc


def near_body(grp_ref, len_ref, gq_ref, kv0_ref, kv1_ref, kv2_ref, mixed_ref):
    for cols, acc in attend_blocks(grp_ref, len_ref, gq_ref, (kv0_ref, kv1_ref, kv2_ref), 0):
        mixed_ref[:, cols] = acc


def last_body(grp_ref, len_ref, tok_ref, gq_ref, part_ref, kv3_ref, gain_ref, wout_ref, out_ref, mixed_ref):
    for cols, acc in attend_blocks(grp_ref, len_ref, gq_ref, (kv3_ref,), 3):
        mixed_ref[:, cols] = part_ref[:, cols] + acc
    gated = (layer_norm(mixed_ref[...], gain_ref[...]) * gq_ref[:, :D].astype(F32)).astype(BF16)
    out_ref[...] = tok_ref[...].astype(F32) + matmul(gated, wout_ref[...])


def attend(grp, lengths, own_tokens, gq, kvs, out_gain, w_out):
    outs = jax.ShapeDtypeStruct((TOK, D), F32)
    part = vmem_call(near_body, outs, n_smem=2, flops=10**9, moved=4 * 2**20, name="attend_near")(
        grp, lengths, gq, *kvs[:3]
    )
    return vmem_call(
        last_body, outs, n_smem=2, scratch=[pltpu.VMEM((TOK, D), F32)], flops=ATTEND_COST, moved=8 * 2**20, name="attend_last"
    )(grp, lengths, own_tokens, gq, part, kvs[3], out_gain, w_out)


def gate_of(u):
    t = jnp.tanh(u)
    return t, jnp.exp(GATE_SCALE * t)


def split(values):
    high = values.astype(BF16).astype(F32)
    return high, values - high


def split_rows(values):
    high, rest = split(values)
    middle, low = split(rest)
    return jnp.concatenate([high, middle, low], 0).astype(BF16)


def loss_body(
    query_ref, near_ref, far_ref, place_ref, back_ref, wqt_ref, wxt_ref,
    loss_ref, qgrad_ref, grads_ref,
    x_ref, unit_ref, cos_ref, dcos_ref, dcosr_ref, side_ref, dqgate_ref, dxgate_ref, dx_ref, du_ref,
):
    lanes = lax.broadcasted_iota(jnp.int32, (NEG + TOK, HALF_ROWS), 1)
    hot_near = (place_ref[...] == lanes).astype(F32).astype(BF16)
    hot_far = (place_ref[...] == lanes + HALF_ROWS).astype(F32).astype(BF16)
    x_ref[...] = (matmul(hot_near, near_ref[...]) + matmul(hot_far, far_ref[...])).astype(BF16)

    part_of = lax.broadcasted_iota(jnp.int32, (16, D), 1) // PW
    pick = (part_of == lax.broadcasted_iota(jnp.int32, (16, D), 0)).astype(F32).astype(BF16)
    eye = lax.broadcasted_iota(jnp.int32, (1, PARTS_SIZE), 1)

    rows = x_ref[...].astype(F32)
    high, low = split(rows * rows)
    squares = matmul_nt(high.astype(BF16), pick) + matmul_nt(low.astype(BF16), pick)
    x_norms = lax.rsqrt(squares[:, :PARTS_SIZE] + 1e-06)
    terms = matmul_nt(x_ref[...], split_rows(wxt_ref[...]))
    xgate = terms[:, :8] + terms[:, 8:16] + terms[:, 16:]
    side = jnp.concatenate([xgate[:NEG], x_norms[:NEG], jnp.zeros((NEG, 112), F32)], 1)
    side_ref[...] = jnp.transpose(side)[:16, :]
    pgate = xgate[NEG:]

    query = query_ref[...]
    qgate = matmul_nt(query, wqt_ref[...], HIGHEST)

    pos_cos = jnp.zeros((TOK, PARTS_SIZE), F32)
    q_norms = []
    for p in range(PARTS_SIZE):
        cols = slice(p * PW, (p + 1) * PW)
        q_p = query_ref[:, cols]
        q_norm = lax.rsqrt(jnp.sum(q_p * q_p, -1, keepdims=True) + 1e-06)
        q_unit = q_p * q_norm
        unit_ref[:, cols] = q_unit
        q_high, q_low = split(q_unit)
        x_p = x_ref[:NEG, cols]
        q_two = jnp.concatenate([q_high.astype(BF16), q_low.astype(BF16)], 1)
        cos_ref[p] = matmul_nt(q_two, jnp.concatenate([x_p, x_p], 1)) * side_ref[8 + p : 9 + p, :]
        dot_p = jnp.sum(q_unit * x_ref[NEG:, cols].astype(F32), -1, keepdims=True)
        pos_cos = jnp.where(eye == p, dot_p, pos_cos)
        q_norms.append(q_norm)
    pos_cos = pos_cos * x_norms[NEG:]

    t_pos, e_pos = gate_of(qgate + pgate)
    mix_pos = e_pos / jnp.sum(e_pos, -1, keepdims=True)
    mean_pos = jnp.sum(mix_pos * pos_cos, -1, keepdims=True)
    pos_logit = INV_TEMP * mean_pos
    raised_pos = jnp.exp(pos_logit)

    dxgate_ref[...] = jnp.zeros_like(dxgate_ref)
    dqgate_ref[...] = qgate
    loss_ref[...] = raised_pos

    def tile(i, carry):
        rows = pl.ds(pl.multiple_of(i * TILE, TILE), TILE)
        qg = dqgate_ref[rows, :]
        qgs = [jnp.broadcast_to(qg[:, p : p + 1], (TILE, PW)) for p in range(PARTS_SIZE)]
        sums = [jnp.zeros((TILE, PW), F32) for _ in range(PARTS_SIZE)]
        part = jnp.zeros((TILE, PW), F32)
        for block in range(NEG // PW):
            cols = slice(block * PW, (block + 1) * PW)
            ts, es, cs = [], [], []
            total = jnp.zeros((TILE, PW), F32)
            mixed = jnp.zeros((TILE, PW), F32)
            for p in range(PARTS_SIZE):
                t, e = gate_of(qgs[p] + side_ref[p : p + 1, cols])
                c = cos_ref[p, rows, cols]
                total = total + e
                mixed = mixed + e * c
                ts.append(t)
                es.append(e)
                cs.append(c)
            inverse = 1.0 / total
            mean = mixed * inverse
            raised = jnp.exp(INV_TEMP * mean)
            part = part + raised
            scaled = raised * inverse
            for p in range(PARTS_SIZE):
                dcos = scaled * es[p]
                du = dcos * (cs[p] - mean) * (1.0 - ts[p] * ts[p])
                dcos_ref[p, rows, cols] = dcos.astype(BF16)
                dcosr_ref[p, rows, cols] = (dcos * side_ref[8 + p : 9 + p, cols]).astype(BF16)
                du_ref[p, :, cols] = du
                sums[p] = sums[p] + du
        partition = loss_ref[rows, :] + jnp.sum(part, -1, keepdims=True)
        factor = (GATE_SCALE * INV_TEMP) / partition
        dq = jnp.zeros((TILE, PARTS_SIZE), F32)
        for p in range(PARTS_SIZE):
            du = du_ref[p] * factor
            dxgate_ref[p] += du[:8] + du[8:]
            dq = jnp.where(eye == p, jnp.sum(sums[p], -1, keepdims=True), dq)
        dqgate_ref[rows, :] = dq * factor
        loss_ref[rows, :] = partition
        return carry

    lax.fori_loop(0, TOK // TILE, tile, 0, unroll=2)

    partition = loss_ref[...]
    loss_ref[...] = jnp.log(partition) - pos_logit
    share = INV_TEMP / partition
    dpos = INV_TEMP * (raised_pos / partition - 1.0)
    dcos_pos = dpos * mix_pos
    du_pos = dcos_pos * (pos_cos - mean_pos) * (GATE_SCALE - GATE_SCALE * t_pos * t_pos)
    dxgate = jnp.transpose(jnp.concatenate([jnp.sum(dxgate_ref[...], 1), jnp.zeros((120, NEG), F32)], 0))

    def by_gate(values):
        high, low = split(values)
        return jnp.concatenate([high, low, high], 1).astype(BF16)

    def gate_weights(values):
        high, low = split(values)
        return jnp.concatenate([high, high, low], 0).astype(BF16)

    dqgate = by_gate(dqgate_ref[...] + du_pos)
    dxgate = by_gate(jnp.concatenate([dxgate[:, :PARTS_SIZE], du_pos], 0))
    wq = gate_weights(wqt_ref[...])
    wx = gate_weights(wxt_ref[...])

    for p in range(PARTS_SIZE):
        cols = slice(p * PW, (p + 1) * PW)
        q_unit = unit_ref[:, cols]
        dc = dcos_pos[:, p : p + 1]
        p_norm = x_norms[NEG:, p : p + 1]
        p_unit = x_ref[NEG:, cols].astype(F32) * p_norm
        d_unit = matmul(dcosr_ref[p], x_ref[:NEG, cols]) * share + dc * p_unit
        along = jnp.sum(d_unit * q_unit, -1, keepdims=True)
        qgrad_ref[:, cols] = (q_norms[p] * (d_unit - q_unit * along) + matmul(dqgate, wq[:, cols])).astype(BF16)

        gate_term = matmul(dxgate, wx[:, cols])
        dpos_p = p_norm * dc * (q_unit - p_unit * pos_cos[:, p : p + 1]) + gate_term[NEG:]
        dx_ref[NEG:, cols] = dpos_p.astype(BF16)

        x_norm = x_norms[:NEG, p : p + 1]
        x_unit = x_ref[:NEG, cols].astype(F32) * x_norm
        d_unit = matmul_tn(dcos_ref[p], (q_unit * share).astype(BF16))
        along = jnp.sum(d_unit * x_unit, -1, keepdims=True)
        dx_ref[:NEG, cols] = (x_norm * (d_unit - x_unit * along) + gate_term[:NEG]).astype(BF16)

    for part in range(4):
        size = 2 * HALF_ROWS // 4
        row = lax.broadcasted_iota(jnp.int32, (size, NEG + TOK), 0) + part * size
        hot = (back_ref[...] == row).astype(F32).astype(BF16)
        grads_ref[part * size : (part + 1) * size, :] = matmul(hot, dx_ref[...]).astype(BF16)


def loss_and_grads(query, near, far, place, back, w_qgate, w_xgate):
    outs = (
        jax.ShapeDtypeStruct((TOK, 1), F32),
        jax.ShapeDtypeStruct((TOK, D), BF16),
        jax.ShapeDtypeStruct((2 * HALF_ROWS, D), BF16),
    )
    scratch = [
        pltpu.VMEM((NEG + TOK, D), BF16),
        pltpu.VMEM((TOK, D), F32),
        pltpu.VMEM((PARTS_SIZE, TOK, NEG), F32),
        pltpu.VMEM((PARTS_SIZE, TOK, NEG), BF16),
        pltpu.VMEM((PARTS_SIZE, TOK, NEG), BF16),
        pltpu.VMEM((2 * PARTS_SIZE, NEG), F32),
        pltpu.VMEM((TOK, PARTS_SIZE), F32),
        pltpu.VMEM((PARTS_SIZE, 8, NEG), F32),
        pltpu.VMEM((NEG + TOK, D), BF16),
        pltpu.VMEM((PARTS_SIZE, TILE, NEG), F32),
    ]
    return vmem_call(loss_body, outs, scratch=scratch, flops=8 * 10**9, moved=10 * 2**20, name="loss")(
        query, near, far, place.reshape(-1, 1), back, w_qgate.T, w_xgate.T
    )


def local(
    tokens,
    lengths,
    in_gain,
    out_gain,
    w_in,
    w_out,
    w_qgate,
    w_xgate,
    item_table,
    neg_owner,
    neg_slot,
    pos_owner,
    pos_slot,
):
    own_tokens = tokens[0]
    half = lax.axis_index("zh").astype(jnp.int32)[None]
    grp = lax.axis_index("grp").astype(jnp.int32)[None]
    barrier = lax.optimization_barrier

    quarter = lax.dynamic_slice_in_dim(item_table, grp[0] * QUARTER, QUARTER, 0)
    tables = lax.all_gather(quarter, COLUMN, tiled=True)

    gate_query, key_value = front_kernel(own_tokens, in_gain[None], w_in)
    kvs = [key_value]
    for _ in range(2):
        kvs.append(lax.ppermute(kvs[-1], "grp", [(i, i + 1) for i in range(3)]))

    half_then, _ = barrier((half, key_value))
    ask, place, back = pack(
        half_then,
        neg_owner.reshape(1, NEG),
        neg_slot.reshape(1, NEG),
        pos_owner.reshape(1, TOK),
        pos_slot.reshape(1, TOK),
    )
    asked = lax.all_to_all(ask, PLANE, split_axis=0, concat_axis=0, tiled=True)

    asked_then, _ = barrier((asked, key_value))
    near_ids = asked_then[:, :CAP].reshape(-1, 1)
    far_ids = asked_then[:, CAP:].reshape(-1, 1)
    looked = look(near_ids, item_table)
    near = lax.all_to_all(looked, PLANE, split_axis=0, concat_axis=0, tiled=True)

    far_ids, _ = barrier((far_ids, kvs[1]))
    far_table = lax.dynamic_slice_in_dim(tables, (1 - half[0]) * ITEMS, ITEMS, 0)
    looked = look(far_ids, far_table, 20)
    far = lax.all_to_all(looked, PLANE, split_axis=0, concat_axis=0, tiled=True)

    kvs[2], _ = barrier((kvs[2], looked))
    kvs.append(lax.ppermute(kvs[2], "grp", [(i, i + 1) for i in range(3)]))
    query = attend(grp, lengths, own_tokens, gate_query, kvs, out_gain[None], w_out)

    losses, query_grad, grads = loss_and_grads(query, near, far, place, back, w_qgate, w_xgate)

    came = lax.all_to_all(grads, PLANE, split_axis=0, concat_axis=0, tiled=True)
    shard = half[0] ^ (lax.broadcasted_iota(jnp.int32, asked.shape, 1) // CAP)
    row = (asked + shard * ITEMS - (half[0] * 4 + grp[0]) * QUARTER) & (2 * ITEMS - 1)
    pieces = add_up(jnp.where(asked >= 0, row, -1).reshape(1, -1), came)
    sums = [ring_sum(pieces[8 * part : 8 * part + 8]) for part in range(len(WIDTHS))]
    return (losses.reshape(1, TOK), query_grad[None], spread(grp, sum((relay(part) for part in sums), [])))


def solution(mesh):
    fine = Mesh(mesh.devices.reshape(4, 4, 2, 4, 2), ("grp", "y", "zh", "x", "core"))
    in_specs = (
        P(SEQ, "grp", None),
        P(SEQ, None),
        P(),
        P(),
        P(),
        P(),
        P(),
        P(),
        P(SEQ, None),
        P(SEQ, "grp", None),
        P(SEQ, "grp"),
        P(SEQ, "grp", None),
        P(SEQ, "grp"),
    )
    out_specs = (P(SEQ, "grp"), P(SEQ, "grp", None), P(SEQ, None))
    return jax.shard_map(local, mesh=fine, in_specs=in_specs, out_specs=out_specs, check_vma=False)
```
